256 devices in a mesh: gx: 8 (over z), gy: 32 (over y, x, core).
Axes of the slice: x: 4, y: 4, z: 8, core: 2. Of those that a mesh axis runs over, the one named last changes fastest.
Arguments:
- probes: float32 [4, 16, 512, 1024], P(None, None, 'gy', 'gx'), may hold values from -6 to 6
- winds: float32 [2, 4, 512, 1024], P(None, None, 'gy', 'gx'), may hold values from -0.4 to 0.4
- diffusivity: float32 [4, 512, 1024], P(None, 'gy', 'gx'), may hold values from 0.04 to 0.15
- mixing: float32 [512, 1024], P('gy', 'gx'), may hold values from 0.02 to 0.2
- prior_scale: float32 [4, 512, 1024], P(None, 'gy', 'gx'), may hold values from 0.3 to 3
- obs_weight: float32 [4, 512, 1024], P(None, 'gy', 'gx'), may hold values from 0.3 to 3
Outputs:
- basis: float32 [4, 16, 512, 1024], P(None, None, 'gy', 'gx')
- factor: float32 [16, 16], replicated
The draws below stay inside these ranges and needn't reach their ends.
All inputs are finite; a program needn't handle non-finite values.
Results may differ from the reference program's by a relative error of at most 0.0003.
Values sent between devices are 32-bit elements; how exact they have to be, the bound alone decides.
No kernel may reach another device: no remote copies, remote signals or barrier semaphores. Data moves between devices by JAX's collectives and lax.ppermute only.
A program may use at most 64 MiB of HBM per device.

```python
import math
import jax
import jax.numpy as jnp
from jax import lax

LEVELS = 4
STEPS = 4
PROBES = 16
NX = 1024
NY = 512
ROWS = 2097152


def draw_probes(key, part):
    key_fields = jax.random.fold_in(key, 11)
    key_mixes = jax.random.fold_in(key, 12)
    key_noise = jax.random.fold_in(key, 13)
    fields = jax.random.normal(key_fields, (4, LEVELS, NY, NX), jnp.float32)
    noise = jax.random.normal(key_noise, (LEVELS, PROBES, NY, NX), jnp.float32)
    mixes = jax.random.normal(key_mixes, (4, PROBES), jnp.float32)
    values = 0.01 * noise
    for index in range(4):
        values = values + 0.5 * fields[index][:, None] * mixes[index][None, :, None, None]
    return jnp.clip(values, -6.0, 6.0)


def levels(rng, dims, split, least, high):
    level, own = 1.0, jax.random.fold_in(rng, 6)
    for position, blocks in split:
        heights = jnp.exp(jax.random.uniform(jax.random.fold_in(own, position), (blocks,), jnp.float32, least / len(split), high / len(split)))
        level = level * jnp.repeat(heights, dims[position] // blocks).reshape([-1 if axis == position else 1 for axis in range(len(dims))])
    return level


def setup_inputs(seed: int = 0) -> dict:
    streams_of = jax.random.split(jax.random.key(seed), 7)
    return {
        "probes": draw_probes(jax.random.fold_in(streams_of[6], 71), 0),
        "winds": jnp.clip(jax.random.uniform(streams_of[1], (2, LEVELS, NY, NX), jnp.float32, -0.4, 0.4) * levels(streams_of[1], (2, LEVELS, NY, NX), ((2, 32), (3, 8)), -0.4, 0.0), -0.4, 0.4),
        "diffusivity": jnp.clip(0.04 + 0.11000001 * jax.random.uniform(streams_of[2], (LEVELS, NY, NX), jnp.float32) ** levels(streams_of[2], (LEVELS, NY, NX), ((1, 32), (2, 8)), -0.2, 0.2), 0.04, 0.15),
        "mixing": jnp.clip(0.02 + 0.18 * jax.random.uniform(streams_of[3], (NY, NX), jnp.float32) ** levels(streams_of[3], (NY, NX), ((0, 32), (1, 8)), -0.2, 0.2), 0.02, 0.2),
        "prior_scale": jnp.clip(jnp.exp(math.log(3.0) - 2.3025851 * jax.random.uniform(streams_of[4], (LEVELS, NY, NX), jnp.float32) ** levels(streams_of[4], (LEVELS, NY, NX), ((1, 32), (2, 8)), -0.2, 0.2)), 0.3, 3.0),
        "obs_weight": jnp.clip(jnp.exp(math.log(3.0) - 2.3025851 * jax.random.uniform(streams_of[5], (LEVELS, NY, NX), jnp.float32) ** levels(streams_of[5], (LEVELS, NY, NX), ((1, 32), (2, 8)), -0.2, 0.2)), 0.3, 3.0),
    }


def vertical(field):
    above = jnp.concatenate([field[1:], field[-1:]], axis=0)
    below = jnp.concatenate([field[:1], field[:-1]], axis=0)
    return above + below - 2.0 * field

def forward_step(extended, coefs):
    center = extended[..., 1:-1, 1:-1]
    east = extended[..., 1:-1, 2:]
    west = extended[..., 1:-1, :-2]
    north = extended[..., 2:, 1:-1]
    south = extended[..., :-2, 1:-1]
    kappa = coefs[0][:, None]
    wind_x = coefs[1][:, None]
    wind_y = coefs[2][:, None]
    rate = coefs[3][:, None]
    return center + kappa * (east + west + north + south - 4.0 * center) - wind_x * (east - west) - wind_y * (north - south) + rate * vertical(center)

def adjoint_step(extended, coefs):
    kappa_g = coefs[0][:, None] * extended
    wind_xg = coefs[1][:, None] * extended
    wind_yg = coefs[2][:, None] * extended
    rate = coefs[3][:, None, 1:-1, 1:-1]
    center = extended[..., 1:-1, 1:-1]
    spread = kappa_g[..., 1:-1, 2:] + kappa_g[..., 1:-1, :-2] + kappa_g[..., 2:, 1:-1] + kappa_g[..., :-2, 1:-1] - 4.0 * kappa_g[..., 1:-1, 1:-1]
    carried = wind_xg[..., 1:-1, 2:] - wind_xg[..., 1:-1, :-2] + wind_yg[..., 2:, 1:-1] - wind_yg[..., :-2, 1:-1]
    return center + spread + carried + rate * vertical(center)

def pad_cells(field):
    return jnp.pad(field, [(0, 0)] * (field.ndim - 2) + [(1, 1), (1, 1)])

def upper_factor(gram):
    count = gram.shape[0]
    positions = jnp.arange(count, dtype=jnp.int32)
    factor_rows = []
    for index in range(count):
        residual_row = gram[index]
        for earlier in factor_rows:
            residual_row = residual_row - earlier[index] * earlier
        pivot = jnp.sqrt(residual_row[index])
        factor_rows.append(jnp.where(positions >= index, residual_row / pivot, jnp.zeros_like(residual_row)))
    return jnp.stack(factor_rows)

def upper_inverse(upper):
    count = upper.shape[0]
    eye = jnp.eye(count, dtype=upper.dtype)
    solved = [None] * count
    for index in range(count - 1, -1, -1):
        row_value = eye[index]
        for later in range(index + 1, count):
            row_value = row_value - upper[index, later] * solved[later]
        solved[index] = row_value / upper[index, index]
    return jnp.stack(solved)

def cholesky_pass(matrix):
    gram = jnp.einsum('lkyx,lmyx->km', matrix, matrix, precision=lax.Precision.HIGHEST)
    upper = upper_factor(gram)
    inverse = upper_inverse(upper)
    result = jnp.einsum('lkyx,km->lmyx', matrix, inverse, precision=lax.Precision.HIGHEST)
    return (result, upper)

def reference(probes, winds, diffusivity, mixing, prior_scale, obs_weight):
    coefs = jnp.stack([diffusivity, winds[0], winds[1], jnp.broadcast_to(mixing, diffusivity.shape)])
    padded_coefs = pad_cells(coefs)
    source = prior_scale[:, None] * probes
    state = jnp.zeros_like(source)
    for step in range(STEPS):
        state = forward_step(pad_cells(state + source), coefs)
    weighted = obs_weight[:, None] * state
    total = jnp.zeros_like(source)
    for step in range(STEPS):
        weighted = adjoint_step(pad_cells(weighted), padded_coefs)
        total = total + weighted
    image = prior_scale[:, None] * total
    first, upper_one = cholesky_pass(image)
    second, upper_two = cholesky_pass(first)
    scale = jnp.sqrt(jnp.float32(ROWS))
    factor = jnp.dot(upper_two, upper_one, precision=lax.Precision.HIGHEST) / scale
    return (second * scale, factor)
```

```python
import math
import jax
import jax.numpy as jnp
from jax import lax
from jax.experimental import pallas as pl
from jax.experimental.pallas import tpu as pltpu
from jax.sharding import PartitionSpec as P

STEPS = 4
LEVELS = 4
PROBES = 16
HALO = 2 * STEPS
LANES = 128
ROWS = 16
EXT = ROWS + 2 * HALO
F32 = jnp.float32

FIELDS = 17
GROUPS = 3
EAST, WEST, NORTH, SOUTH, CENTER, RATE, OBS, DERIVED = 0, 4, 8, 12, 16, 20, 21, 25
X_PARTS = ROWS + 2 * GROUPS
Y_SOURCE, Y_HALO, Y_COEF, Y_COEF_HALO, Y_PARTS = 0, 64, 72, 89, 92
SLICES = 4


def lane_ids():
    return lax.broadcasted_iota(jnp.int32, (8, LANES), 1)


def roll_lanes(value, shift):
    shift = shift % LANES
    return value if shift == 0 else pltpu.roll(value, shift, value.ndim - 1)


def raw_field(refs, field, rows):
    diffusivity, winds, obs, mixing = refs
    if field < 4:
        return diffusivity[field, rows, :]
    if field < 8:
        return winds[0, field - 4, rows, :]
    if field < 12:
        return winds[1, field - 8, rows, :]
    if field < 16:
        return obs[field - 12, rows, :]
    return mixing[rows, :]


def pack_kernel(probes, winds, diffusivity, mixing, prior, obs, source, east, west):
    lanes = lane_ids()
    half = lanes // 8

    def put(held, value, slot):
        to_east, to_west = held
        to_east = jnp.where(half == 2 * slot + 1, roll_lanes(value, 16 * slot + 8 - (LANES - HALO)), to_east)
        to_west = jnp.where(half == 2 * slot, roll_lanes(value, 16 * slot), to_west)
        return to_east, to_west

    zero = jnp.zeros((8, LANES), F32)

    def row(y, carry):
        held = (zero, zero)
        for level in range(LEVELS):
            scale = prior[level, pl.ds(y, 1), :]
            for part in range(2):
                value = probes[level, pl.ds(part * 8 * ROWS + y, 8, stride=ROWS), :] * scale
                source[y, level, part] = value
                held = put(held, value, 2 * level + part)
        east[y], west[y] = held
        return carry

    lax.fori_loop(0, ROWS, row, 0, unroll=2)
    refs = (diffusivity, winds, obs, mixing)
    for group in range(GROUPS):
        for tile in range(2):
            held = (zero, zero)
            for slot in range(8):
                field = 8 * group + slot
                if field < FIELDS:
                    held = put(held, raw_field(refs, field, pl.ds(8 * tile, 8)), slot)
            east[ROWS + 2 * group + tile], west[ROWS + 2 * group + tile] = held


def merge_kernel(from_west, from_east, source, winds, diffusivity, mixing, obs, halo, north, south):
    inner = lane_ids() % 16 < 8
    for index in range(X_PARTS):
        halo[index] = jnp.where(inner, from_east[index], from_west[index])
    refs = (diffusivity, winds, obs, mixing)
    for tile, out in ((0, south), (1, north)):
        for y in range(8):
            for level in range(LEVELS):
                for part in range(2):
                    out[(y * LEVELS + level) * 2 + part] = source[8 * tile + y, level, part]
            out[Y_HALO + y] = jnp.where(inner, from_east[8 * tile + y], from_west[8 * tile + y])
        for field in range(FIELDS):
            out[Y_COEF + field] = raw_field(refs, field, pl.ds(8 * tile, 8))
        for group in range(GROUPS):
            index = ROWS + 2 * group + tile
            out[Y_COEF_HALO + group] = jnp.where(inner, from_east[index], from_west[index])


def strip_of(lanes, first, second, halo_first, halo_second, slot_first, slot_second):
    value = roll_lanes(first, 24)
    value = jnp.where(lanes >= 24, roll_lanes(halo_first, 24 - 16 * slot_first), value)
    value = jnp.where(lanes >= 40, roll_lanes(first, 40), value)
    value = jnp.where(lanes >= 64, roll_lanes(second, 88), value)
    value = jnp.where(lanes >= 88, roll_lanes(halo_second, 88 - 16 * slot_second), value)
    return jnp.where(lanes >= 104, roll_lanes(second, 104), value)


def two_sum(a, b):
    total = a + b
    other = total - a
    return total, (a - (total - other)) + (b - other)


def stencil_kernel(
    source, halo, winds, diffusivity, mixing, prior, obs, from_south, from_north,
    image, message, start, first, second, adjoints, coefs, slices,
):
    lanes = lane_ids()
    refs = (diffusivity, winds, obs, mixing)

    for tile in range(4):
        if tile in (1, 2):
            main = [raw_field(refs, field, pl.ds(8 * (tile - 1), 8)) for field in range(FIELDS)]
            packed = [halo[ROWS + 2 * group + tile - 1] for group in range(GROUPS)]
        else:
            ref = from_south if tile == 0 else from_north
            main = [ref[Y_COEF + field] for field in range(FIELDS)]
            packed = [ref[Y_COEF_HALO + group] for group in range(GROUPS)]
        strips = [
            strip_of(lanes, main[field], main[field], packed[field // 8], packed[field // 8], field % 8, field % 8)
            for field in range(FIELDS)
        ]
        rows = pl.ds(8 * tile, 8)
        for kind, values in ((0, main), (1, strips)):
            rate = values[16]
            coefs[kind, RATE, rows, :] = rate
            for level in range(LEVELS):
                kappa, wind_x, wind_y = values[level], values[4 + level], values[8 + level]
                coefs[kind, EAST + level, rows, :] = kappa - wind_x
                coefs[kind, WEST + level, rows, :] = kappa + wind_x
                coefs[kind, NORTH + level, rows, :] = kappa - wind_y
                coefs[kind, SOUTH + level, rows, :] = kappa + wind_y
                sides = 1.0 if level in (0, LEVELS - 1) else 2.0
                coefs[kind, CENTER + level, rows, :] = 1.0 - 4.0 * kappa - sides * rate
                coefs[kind, OBS + level, rows, :] = values[12 + level]

    def load_rows(get, get_halo, base):
        def row(y, carry):
            packed = get_halo(y)
            for level in range(LEVELS):
                low, high = get(y, level, 0), get(y, level, 1)
                start[base + y, level, 0] = low
                start[base + y, level, 1] = high
                start[base + y, level, 2] = strip_of(lanes, low, high, packed, packed, 2 * level, 2 * level + 1)
            return carry
        return row

    def beside(ref):
        return (lambda y, level, part: ref[(y * LEVELS + level) * 2 + part]), (lambda y: ref[Y_HALO + y])

    lax.fori_loop(0, HALO, load_rows(*beside(from_south), 0), 0)
    lax.fori_loop(0, ROWS, load_rows(lambda y, level, part: source[y, level, part], lambda y: halo[y], HALO), 0)
    lax.fori_loop(0, HALO, load_rows(*beside(from_north), HALO + ROWS), 0)

    def vertical(values, level):
        if level == 0:
            return values[1]
        if level == LEVELS - 1:
            return values[LEVELS - 2]
        return values[level - 1] + values[level + 1]

    def forward(ref, y, part):
        kind = part // 2
        coef = lambda index: coefs[kind, index, pl.ds(y, 1), :]
        center = [ref[y, level, part] for level in range(LEVELS)]
        rate = coef(RATE)
        out = []
        for level in range(LEVELS):
            value = center[level]
            out.append(
                coef(CENTER + level) * value
                + coef(EAST + level) * roll_lanes(value, -1)
                + coef(WEST + level) * roll_lanes(value, 1)
                + coef(NORTH + level) * ref[y + 1, level, part]
                + coef(SOUTH + level) * ref[y - 1, level, part]
                + rate * vertical(center, level)
            )
        return out

    def adjoint(ref, y, part):
        kind = part // 2
        coef = lambda index, at: coefs[kind, index, pl.ds(at, 1), :]
        center = [ref[y, level, part] for level in range(LEVELS)]
        rate = coef(RATE, y)
        out = []
        for level in range(LEVELS):
            value = center[level]
            out.append(
                coef(CENTER + level, y) * value
                + roll_lanes(coef(WEST + level, y) * value, -1)
                + roll_lanes(coef(EAST + level, y) * value, 1)
                + coef(SOUTH + level, y + 1) * ref[y + 1, level, part]
                + coef(NORTH + level, y - 1) * ref[y - 1, level, part]
                + rate * vertical(center, level)
            )
        return out

    held = [start, first, second, first, second]
    for step in range(1, STEPS + 1):
        def row(y, carry, step=step):
            for part in range(3):
                values = forward(held[step - 1], y, part)
                for level in range(LEVELS):
                    if step < STEPS:
                        value = values[level] + start[y, level, part]
                    else:
                        value = values[level] * coefs[part // 2, OBS + level, pl.ds(y, 1), :]
                    held[step][y, level, part] = value
            return carry
        lax.fori_loop(step, EXT - step, row, 0)

    held = [second] + [adjoints.at[index] for index in range(STEPS - 1)]
    for step in range(1, STEPS):
        def row(y, carry, step=step):
            for part in range(3):
                values = adjoint(held[step - 1], y, part)
                for level in range(LEVELS):
                    held[step][y, level, part] = values[level]
            return carry
        lax.fori_loop(STEPS + step, EXT - STEPS - step, row, 0)

    def last_row(y, most):
        totals = []
        for part in range(3):
            values = adjoint(held[STEPS - 1], y, part)
            totals.append([
                values[level] + held[1][y, level, part] + held[2][y, level, part] + held[3][y, level, part]
                for level in range(LEVELS)
            ])
        most = list(most)
        for level in range(LEVELS):
            scale = prior[level, pl.ds(y - HALO, 1), :]
            strip = totals[2][level]
            for part in range(2):
                value = jnp.where(lanes < HALO, roll_lanes(strip, -40 - 64 * part), totals[part][level])
                value = jnp.where(lanes >= LANES - HALO, roll_lanes(strip, 104 - 64 * part), value)
                value = value * scale
                image[y - HALO, level, part] = value
                most[part] = jnp.maximum(most[part], jnp.abs(value))
        return tuple(most)

    zero = jnp.zeros((8, LANES), F32)
    most = lax.fori_loop(HALO, HALO + ROWS, last_row, (zero, zero))

    magics = []
    for part in range(2):
        top = jnp.broadcast_to(jnp.max(most[part], axis=1, keepdims=True), (8, LANES))
        scaled = top * (2.0**23 + 1.0)
        power = jnp.abs(scaled - scaled * (1.0 - 2.0**-24))
        magics.append([power * (1.5 * 2.0 ** (23 - 6 - 8 * index)) for index in range(SLICES)])

    def slice_row(y, carry):
        for level in range(LEVELS):
            pieces = []
            for part in range(2):
                rest = image[y, level, part]
                own = []
                for index in range(SLICES):
                    magic = magics[part][index]
                    piece = (rest + magic) - magic
                    rest = rest - piece
                    own.append(piece)
                pieces.append(own)
            for index in range(SLICES):
                both = jnp.concatenate([pieces[0][index], pieces[1][index]], axis=0)
                slices[y, pl.ds(PROBES * index, PROBES), pl.ds(LANES * level, LANES)] = both.astype(jnp.bfloat16)
        return carry

    lax.fori_loop(0, ROWS, slice_row, 0)

    width = PROBES * SLICES
    high = jnp.zeros((width, width), F32)
    low = jnp.zeros((width, width), F32)
    for pair in range(ROWS // 2):
        block = jnp.concatenate([slices[2 * pair], slices[2 * pair + 1]], axis=1)
        product = lax.dot_general(block, block, (((1,), (1,)), ((), ())), preferred_element_type=F32)
        high, error = two_sum(high, product)
        low = low + error

    def fold(high, low, blocks):
        total_high, total_low = None, None
        for block_high, block_low in blocks(high, low):
            if total_high is None:
                total_high, total_low = block_high, block_low
            else:
                total_high, error = two_sum(total_high, block_high)
                total_low = total_low + block_low + error
        return total_high, total_low

    def row_blocks(high, low):
        for index in range(SLICES):
            rows = slice(PROBES * index, PROBES * (index + 1))
            yield high[rows], low[rows]

    def lane_blocks(high, low):
        for index in range(SLICES):
            yield roll_lanes(high, -PROBES * index), roll_lanes(low, -PROBES * index)

    high, low = fold(high, low, row_blocks)
    rest = jnp.zeros((PROBES, LANES - width), F32)
    high, low = jnp.concatenate([high, rest], axis=1), jnp.concatenate([low, rest], axis=1)
    high, low = fold(high, low, lane_blocks)
    high, low = two_sum(high, low)

    wide = lax.broadcasted_iota(jnp.int32, (PROBES, LANES), 1)
    both = jnp.where(wide < PROBES, high, roll_lanes(low, PROBES))
    packed = both[0:8]
    for index in range(1, 4):
        value = both[8 * (index // 2) : 8 * (index // 2) + 8]
        if index % 2:
            value = pltpu.roll(value, 4, 0)
        packed = jnp.where(lanes // 32 == index, roll_lanes(value, 32 * index), packed)
    message[...] = jnp.broadcast_to(packed[None, 0:4], message.shape)


def split(a):
    scaled = a * 4097.0
    high = scaled - (scaled - a)
    return high, a - high


def product_error(a, b, product):
    a_high, a_low = a
    b_high, b_low = b
    return ((a_high * b_high - product) + a_high * b_low + a_low * b_high) + a_low * b_low


def factor_kernel(count, received, image, basis, factor):
    lanes = lane_ids()
    upper_half = lax.broadcasted_iota(jnp.int32, (8, LANES), 0) < 4
    zero = jnp.zeros((8, LANES), F32)
    chains = 4

    def add(index, carry):
        sums, errors = carry
        new_sums, new_errors = [], []
        for chain in range(chains):
            total, error = two_sum(sums[chain], received[index * chains + chain])
            new_sums.append(total)
            new_errors.append(errors[chain] + error)
        return tuple(new_sums), tuple(new_errors)

    sums, errors = lax.fori_loop(0, received.shape[0] // chains, add, ((zero,) * chains, (zero,) * chains), unroll=4)
    total, rest = sums[0], errors[0]
    for chain in range(1, chains):
        total, error = two_sum(total, sums[chain])
        rest = rest + errors[chain] + error
    total, error = two_sum(total, pltpu.roll(total, 4, 0))
    rest = rest + pltpu.roll(rest, 4, 0) + error
    rest = rest + roll_lanes(total, -PROBES)

    def unpack(value):
        low = jnp.where(upper_half, value, roll_lanes(value, -32))
        high = jnp.where(upper_half, roll_lanes(value, -64), roll_lanes(value, -96))
        return jnp.concatenate([low, high], axis=0)

    high, low = two_sum(unpack(total), unpack(rest))

    shape = (PROBES, LANES)
    wide = lax.broadcasted_iota(jnp.int32, shape, 1)
    rows = lax.broadcasted_iota(jnp.int32, shape, 0)
    high = jnp.where(wide < PROBES, high, jnp.where(wide == rows + PROBES, 1.0, 0.0))
    low = jnp.where(wide < PROBES, low, 0.0)
    for step in range(PROBES - 1):
        row_high = jnp.broadcast_to(high[step : step + 1], shape)
        row_low = jnp.broadcast_to(low[step : step + 1], shape)
        column_high = jnp.broadcast_to(high[:, step : step + 1], shape)
        column_low = jnp.broadcast_to(low[:, step : step + 1], shape)
        pivot_high = jnp.broadcast_to(row_high[:, step : step + 1], shape)
        pivot_low = jnp.broadcast_to(row_low[:, step : step + 1], shape)
        inverse = 1.0 / pivot_high
        ratio = jnp.where(rows > step, column_high * inverse, 0.0)
        ratio_parts = split(ratio)
        taken = ratio * pivot_high
        remainder = ((column_high - taken) - product_error(ratio_parts, split(pivot_high), taken)) + (
            column_low - ratio * pivot_low
        )
        ratio_low = jnp.where(rows > step, remainder * inverse, 0.0)
        taken = ratio * row_high
        taken_error = product_error(ratio_parts, split(row_high), taken)
        high, error = two_sum(high, -taken)
        low = low + error - taken_error - (ratio * row_low + ratio_low * row_high)
        high, low = two_sum(high, low)

    diagonal = jnp.sum(jnp.where(wide == rows, high, 0.0), axis=1, keepdims=True)
    root = jnp.broadcast_to(jnp.sqrt(diagonal), shape)
    size = math.sqrt(count)
    upper = high / root
    factor[...] = jnp.where(wide >= rows, upper * (1.0 / size), 0.0)[:, :PROBES]
    inverse = upper * size
    columns = [
        jnp.broadcast_to(inverse[:, PROBES + index : PROBES + index + 1], shape) for index in range(PROBES)
    ]

    def row(y, carry):
        for level in range(LEVELS):
            outs = [None, None]
            for index in range(PROBES):
                value = image[y, level, index // 8, pl.ds(index % 8, 1), :]
                for part in range(index // 8, 2):
                    term = columns[index][8 * part : 8 * part + 8] * value
                    outs[part] = term if outs[part] is None else outs[part] + term
            for part in range(2):
                basis[level, pl.ds(part * 8 * ROWS + y, 8, stride=ROWS), :] = outs[part]
        return carry

    lax.fori_loop(0, ROWS, row, 0)


def call(kernel, outs, scratch=()):
    vmem = pl.BlockSpec(memory_space=pltpu.VMEM)

    def run(*operands):
        return pl.pallas_call(
            kernel,
            out_shape=[jax.ShapeDtypeStruct(shape, F32) for shape in outs],
            in_specs=[vmem] * len(operands),
            out_specs=[vmem] * len(outs),
            scratch_shapes=list(scratch),
            compiler_params=pltpu.CompilerParams(vmem_limit_bytes=40 << 20),
        )(*operands)

    return run


def body(probes, winds, diffusivity, mixing, prior_scale, obs_weight):
    tile = (8, LANES)
    size_x, size_y = lax.axis_size("gx"), lax.axis_size("gy")
    devices = size_x * size_y
    count = LEVELS * ROWS * LANES * devices

    def shift(value, axis, step):
        number = lax.axis_size(axis)
        pairs = [(i, i + step) for i in range(number) if 0 <= i + step < number]
        return lax.ppermute(value, axis, pairs)

    flat = probes.reshape(LEVELS, PROBES * ROWS, LANES)
    source, east, west = call(
        pack_kernel, [(ROWS, LEVELS, 2) + tile, (X_PARTS,) + tile, (X_PARTS,) + tile]
    )(flat, winds, diffusivity, mixing, prior_scale, obs_weight)
    from_west = shift(east, "gx", 1)
    from_east = shift(west, "gx", -1)
    halo, north, south = call(
        merge_kernel, [(X_PARTS,) + tile, (Y_PARTS,) + tile, (Y_PARTS,) + tile]
    )(from_west, from_east, source, winds, diffusivity, mixing, obs_weight)
    from_south = shift(north, "gy", 1)
    from_north = shift(south, "gy", -1)
    field = (EXT, LEVELS, 3) + tile
    image, message = call(
        stencil_kernel,
        [(ROWS, LEVELS, 2) + tile, (devices, 4, LANES)],
        [
            pltpu.VMEM(field, F32),
            pltpu.VMEM(field, F32),
            pltpu.VMEM(field, F32),
            pltpu.VMEM((STEPS - 1,) + field, F32),
            pltpu.VMEM((2, DERIVED, EXT, LANES), F32),
            pltpu.VMEM((ROWS, PROBES * SLICES, LEVELS * LANES), jnp.bfloat16),
        ],
    )(source, halo, winds, diffusivity, mixing, prior_scale, obs_weight, from_south, from_north)
    received = lax.all_to_all(message, ("gx", "gy"), 0, 0)
    received = received.reshape((devices // 2,) + tile)
    basis, factor = call(
        lambda *refs: factor_kernel(count, *refs),
        [(LEVELS, PROBES * ROWS, LANES), (PROBES, PROBES)],
    )(received, image)
    return basis.reshape(probes.shape), factor


def solution(mesh):
    placed = (
        P(None, None, "gy", "gx"),
        P(None, None, "gy", "gx"),
        P(None, "gy", "gx"),
        P("gy", "gx"),
        P(None, "gy", "gx"),
        P(None, "gy", "gx"),
    )
    return jax.shard_map(
        body,
        mesh=mesh,
        in_specs=placed,
        out_specs=(P(None, None, "gy", "gx"), P()),
        check_vma=False,
    )
```

```python
import math
import jax
import jax.numpy as jnp
from jax import lax
from jax.experimental import pallas as pl
from jax.experimental.pallas import tpu as pltpu
from jax.sharding import PartitionSpec as P

STEPS = 4
LEVELS = 4
PROBES = 16
HALO = 2 * STEPS
LANES = 128
ROWS = 16
EXT = ROWS + 2 * HALO
F32 = jnp.float32

FIELDS = 17
GROUPS = 3
EAST, WEST, NORTH, SOUTH, CENTER, RATE, OBS, DERIVED = 0, 4, 8, 12, 16, 20, 21, 25
X_PARTS = ROWS + 2 * GROUPS
Y_SOURCE, Y_HALO, Y_COEF, Y_COEF_HALO, Y_PARTS = 0, 64, 72, 89, 92
SLICES = 4


def lane_ids():
    return lax.broadcasted_iota(jnp.int32, (8, LANES), 1)


def roll_lanes(value, shift):
    shift = shift % LANES
    return value if shift == 0 else pltpu.roll(value, shift, value.ndim - 1)


def pack_kernel(
    probes_in, winds_in, diffusivity_in, mixing_in, prior_in, obs_in,
    source, east, west, fields, prior, probes, sems,
):
    coef_copies = [
        pltpu.make_async_copy(diffusivity_in, fields.at[pl.ds(0, 4)], sems.at[0]),
        pltpu.make_async_copy(winds_in.at[0], fields.at[pl.ds(4, 4)], sems.at[1]),
        pltpu.make_async_copy(winds_in.at[1], fields.at[pl.ds(8, 4)], sems.at[2]),
        pltpu.make_async_copy(obs_in, fields.at[pl.ds(12, 4)], sems.at[3]),
        pltpu.make_async_copy(mixing_in, fields.at[16], sems.at[4]),
    ]
    source_copies = [
        pltpu.make_async_copy(probes_in, probes, sems.at[5]),
        pltpu.make_async_copy(prior_in, prior, sems.at[6]),
    ]
    for copy in source_copies + coef_copies:
        copy.start()
    lanes = lane_ids()
    half = lanes // 8

    def put(held, value, slot):
        to_east, to_west = held
        to_east = jnp.where(half == 2 * slot + 1, roll_lanes(value, 16 * slot + 8 - (LANES - HALO)), to_east)
        to_west = jnp.where(half == 2 * slot, roll_lanes(value, 16 * slot), to_west)
        return to_east, to_west

    zero = jnp.zeros((8, LANES), F32)

    def row(y, carry):
        held = (zero, zero)
        for level in range(LEVELS):
            scale = prior[level, pl.ds(y, 1), :]
            for part in range(2):
                value = probes[level, pl.ds(part * 8 * ROWS + y, 8, stride=ROWS), :] * scale
                source[y, level, part] = value
                held = put(held, value, 2 * level + part)
        east[y], west[y] = held
        return carry

    for copy in coef_copies:
        copy.wait()
    for group in range(GROUPS):
        for tile in range(2):
            held = (zero, zero)
            for slot in range(8):
                field = 8 * group + slot
                if field < FIELDS:
                    held = put(held, fields[field, pl.ds(8 * tile, 8), :], slot)
            east[ROWS + 2 * group + tile], west[ROWS + 2 * group + tile] = held
    for copy in source_copies:
        copy.wait()
    lax.fori_loop(0, ROWS, row, 0, unroll=True)


def merge_kernel(from_west, from_east, source, fields, halo, north, south):
    inner = lane_ids() % 16 < 8
    for index in range(X_PARTS):
        halo[index] = jnp.where(inner, from_east[index], from_west[index])
    for tile, out in ((0, south), (1, north)):
        for y in range(8):
            for level in range(LEVELS):
                for part in range(2):
                    out[(y * LEVELS + level) * 2 + part] = source[8 * tile + y, level, part]
            out[Y_HALO + y] = jnp.where(inner, from_east[8 * tile + y], from_west[8 * tile + y])
        for field in range(FIELDS):
            out[Y_COEF + field] = fields[field, pl.ds(8 * tile, 8), :]
        for group in range(GROUPS):
            index = ROWS + 2 * group + tile
            out[Y_COEF_HALO + group] = jnp.where(inner, from_east[index], from_west[index])


def strip_of(lanes, first, second, halo_first, halo_second, slot_first, slot_second):
    value = roll_lanes(first, 24)
    value = jnp.where(lanes >= 24, roll_lanes(halo_first, 24 - 16 * slot_first), value)
    value = jnp.where(lanes >= 40, roll_lanes(first, 40), value)
    value = jnp.where(lanes >= 64, roll_lanes(second, 88), value)
    value = jnp.where(lanes >= 88, roll_lanes(halo_second, 88 - 16 * slot_second), value)
    return jnp.where(lanes >= 104, roll_lanes(second, 104), value)


def two_sum(a, b):
    total = a + b
    other = total - a
    return total, (a - (total - other)) + (b - other)


def stencil_kernel(
    source, halo, fields, prior, from_south, from_north,
    image, message, start, first, second, adjoints, coefs, slices,
):
    lanes = lane_ids()

    for tile in range(4):
        if tile in (1, 2):
            main = [fields[field, pl.ds(8 * (tile - 1), 8), :] for field in range(FIELDS)]
            packed = [halo[ROWS + 2 * group + tile - 1] for group in range(GROUPS)]
        else:
            ref = from_south if tile == 0 else from_north
            main = [ref[Y_COEF + field] for field in range(FIELDS)]
            packed = [ref[Y_COEF_HALO + group] for group in range(GROUPS)]
        strips = [
            strip_of(lanes, main[field], main[field], packed[field // 8], packed[field // 8], field % 8, field % 8)
            for field in range(FIELDS)
        ]
        rows = pl.ds(8 * tile, 8)
        for kind, values in ((0, main), (1, strips)):
            rate = values[16]
            coefs[kind, RATE, rows, :] = rate
            for level in range(LEVELS):
                kappa, wind_x, wind_y = values[level], values[4 + level], values[8 + level]
                coefs[kind, EAST + level, rows, :] = kappa - wind_x
                coefs[kind, WEST + level, rows, :] = kappa + wind_x
                coefs[kind, NORTH + level, rows, :] = kappa - wind_y
                coefs[kind, SOUTH + level, rows, :] = kappa + wind_y
                sides = 1.0 if level in (0, LEVELS - 1) else 2.0
                coefs[kind, CENTER + level, rows, :] = 1.0 - 4.0 * kappa - sides * rate
                coefs[kind, OBS + level, rows, :] = values[12 + level]

    def load_rows(get, get_halo, base):
        def row(y, carry):
            packed = get_halo(y)
            for level in range(LEVELS):
                low, high = get(y, level, 0), get(y, level, 1)
                start[base + y, level, 0] = low
                start[base + y, level, 1] = high
                start[base + y, level, 2] = strip_of(lanes, low, high, packed, packed, 2 * level, 2 * level + 1)
            return carry
        return row

    def beside(ref):
        return (lambda y, level, part: ref[(y * LEVELS + level) * 2 + part]), (lambda y: ref[Y_HALO + y])

    lax.fori_loop(0, HALO, load_rows(*beside(from_south), 0), 0, unroll=True)
    lax.fori_loop(0, ROWS, load_rows(lambda y, level, part: source[y, level, part], lambda y: halo[y], HALO), 0, unroll=True)
    lax.fori_loop(0, HALO, load_rows(*beside(from_north), HALO + ROWS), 0, unroll=True)

    def vertical(values, level):
        if level == 0:
            return values[1]
        if level == LEVELS - 1:
            return values[LEVELS - 2]
        return values[level - 1] + values[level + 1]

    def coefs_at(kind, y):
        return lambda index: coefs[kind, index, pl.ds(y, 1), :]

    def load(ref, y, parts):
        return tuple(tuple(ref[y, level, part] for level in range(LEVELS)) for part in parts)

    def forward(ref, low, high, parts, emit):
        def row(y, carry):
            before, center = carry
            after = load(ref, y + 1, parts)
            coef = coefs_at(parts[0] // 2, y)
            rate = coef(RATE)
            own = [[coef(base + level) for base in (CENTER, EAST, WEST, NORTH, SOUTH)] for level in range(LEVELS)]
            results = []
            for index in range(len(parts)):
                values = []
                for level in range(LEVELS):
                    value = center[index][level]
                    middle, east, west, north, south = own[level]
                    values.append(
                        (middle * value + rate * vertical(center[index], level))
                        + (north * after[index][level] + south * before[index][level])
                        + (east * roll_lanes(value, -1) + west * roll_lanes(value, 1))
                    )
                results.append(values)
            emit(y, parts, coef, results)
            return center, after

        lax.fori_loop(low, high, row, (load(ref, low - 1, parts), load(ref, low, parts)), unroll=True)

    def adjoint(ref, low, high, parts, emit, state):
        def spread(y, pushed):
            center = load(ref, y, parts)
            coef = coefs_at(parts[0] // 2, y)
            rate = coef(RATE)
            own = [[coef(base + level) for base in (CENTER, EAST, WEST, NORTH)] for level in range(LEVELS)]
            partial, push = [], []
            for index in range(len(parts)):
                values, pushes = [], []
                for level in range(LEVELS):
                    value = center[index][level]
                    middle, east, west, north = own[level]
                    values.append(
                        (middle * value + rate * vertical(center[index], level))
                        + (roll_lanes(west * value, -1) + roll_lanes(east * value, 1))
                        + pushed[index][level]
                    )
                    pushes.append(north * value)
                partial.append(tuple(values))
                push.append(tuple(pushes))
            return center, tuple(partial), tuple(push)

        def pull(y, center, partial):
            coef = coefs_at(parts[0] // 2, y)
            south = [coef(SOUTH + level) for level in range(LEVELS)]
            return [
                [partial[index][level] + south[level] * center[index][level] for level in range(LEVELS)]
                for index in range(len(parts))
            ]

        below = load(ref, low - 1, parts)
        coef = coefs_at(parts[0] // 2, low - 1)
        north = [coef(NORTH + level) for level in range(LEVELS)]
        push = tuple(tuple(north[level] * values[level] for level in range(LEVELS)) for values in below)
        center, partial, push = spread(low, push)

        def row(y, carry):
            partial, push, state = carry
            center, new_partial, push = spread(y + 1, push)
            state = emit(y, parts, pull(y + 1, center, partial), state)
            return new_partial, push, state

        partial, push, state = lax.fori_loop(low, high - 1, row, (partial, push, state), unroll=True)
        return emit(high - 1, parts, pull(high, load(ref, high, parts), partial), state)

    groups = ((2,), (0, 1))
    held = [start, first, second, first, second]
    for step in range(1, STEPS + 1):
        def emit(y, parts, coef, results, step=step):
            for level in range(LEVELS):
                for index, part in enumerate(parts):
                    value = results[index][level]
                    if step < STEPS:
                        value = value + start[y, level, part]
                    else:
                        value = value * coef(OBS + level)
                    held[step][y, level, part] = value

        for parts in groups:
            forward(held[step - 1], step, EXT - step, parts, emit)

    held = [second] + [adjoints.at[index] for index in range(STEPS - 1)]
    for step in range(1, STEPS):
        def emit(y, parts, results, state, step=step):
            for index, part in enumerate(parts):
                for level in range(LEVELS):
                    held[step][y, level, part] = results[index][level]
            return state

        for parts in groups:
            adjoint(held[step - 1], STEPS + step, EXT - STEPS - step, parts, emit, ())

    def total_of(y, part, level, value):
        return (held[1][y, level, part] + held[2][y, level, part]) + (held[3][y, level, part] + value)

    def emit_strip(y, parts, results, state):
        for level in range(LEVELS):
            first[y, level, 2] = total_of(y, 2, level, results[0][level])
        return state

    def emit_image(y, parts, results, most):
        most = list(most)
        for level in range(LEVELS):
            scale = prior[level, pl.ds(y - HALO, 1), :]
            strip = first[y, level, 2]
            for part in range(2):
                value = total_of(y, part, level, results[part][level])
                value = jnp.where(lanes < HALO, roll_lanes(strip, -40 - 64 * part), value)
                value = jnp.where(lanes >= LANES - HALO, roll_lanes(strip, 104 - 64 * part), value)
                value = value * scale
                image[y - HALO, level, part] = value
                most[part] = jnp.maximum(most[part], jnp.abs(value))
        return tuple(most)

    zero = jnp.zeros((8, LANES), F32)
    adjoint(held[STEPS - 1], HALO, HALO + ROWS, (2,), emit_strip, ())
    most = adjoint(held[STEPS - 1], HALO, HALO + ROWS, (0, 1), emit_image, (zero, zero))

    magics = []
    for part in range(2):
        top = jnp.broadcast_to(jnp.max(most[part], axis=1, keepdims=True), (8, LANES))
        scaled = top * (2.0**23 + 1.0)
        power = jnp.abs(scaled - scaled * (1.0 - 2.0**-24))
        magics.append([power * (1.5 * 2.0 ** (23 - 6 - 8 * index)) for index in range(SLICES)])

    def slice_row(y, carry):
        for level in range(LEVELS):
            pieces = []
            for part in range(2):
                rest = image[y, level, part]
                own = []
                for index in range(SLICES):
                    magic = magics[part][index]
                    piece = (rest + magic) - magic
                    rest = rest - piece
                    own.append(piece)
                pieces.append(own)
            for index in range(SLICES):
                both = jnp.concatenate([pieces[0][index], pieces[1][index]], axis=0)
                slices[y, pl.ds(PROBES * index, PROBES), pl.ds(LANES * level, LANES)] = both.astype(jnp.bfloat16)
        return carry

    lax.fori_loop(0, ROWS, slice_row, 0, unroll=True)

    width = PROBES * SLICES
    high = jnp.zeros((width, width), F32)
    low = jnp.zeros((width, width), F32)
    for pair in range(ROWS // 2):
        block = jnp.concatenate([slices[2 * pair], slices[2 * pair + 1]], axis=1)
        product = lax.dot_general(block, block, (((1,), (1,)), ((), ())), preferred_element_type=F32)
        high, error = two_sum(high, product)
        low = low + error

    def fold(high, low, blocks):
        total_high, total_low = None, None
        for block_high, block_low in blocks(high, low):
            if total_high is None:
                total_high, total_low = block_high, block_low
            else:
                total_high, error = two_sum(total_high, block_high)
                total_low = total_low + block_low + error
        return total_high, total_low

    def row_blocks(high, low):
        for index in range(SLICES):
            rows = slice(PROBES * index, PROBES * (index + 1))
            yield high[rows], low[rows]

    def lane_blocks(high, low):
        for index in range(SLICES):
            yield roll_lanes(high, -PROBES * index), roll_lanes(low, -PROBES * index)

    high, low = fold(high, low, row_blocks)
    rest = jnp.zeros((PROBES, LANES - width), F32)
    high, low = jnp.concatenate([high, rest], axis=1), jnp.concatenate([low, rest], axis=1)
    high, low = fold(high, low, lane_blocks)
    high, low = two_sum(high, low)

    wide = lax.broadcasted_iota(jnp.int32, (PROBES, LANES), 1)
    both = jnp.where(wide < PROBES, high, roll_lanes(low, PROBES))
    packed = both[0:8]
    for index in range(1, 4):
        value = both[8 * (index // 2) : 8 * (index // 2) + 8]
        if index % 2:
            value = pltpu.roll(value, 4, 0)
        packed = jnp.where(lanes // 32 == index, roll_lanes(value, 32 * index), packed)
    message[...] = jnp.broadcast_to(packed[None, 0:4], message.shape)


def split(a):
    scaled = a * 4097.0
    high = scaled - (scaled - a)
    return high, a - high


def product_error(a, b, product):
    a_high, a_low = a
    b_high, b_low = b
    return ((a_high * b_high - product) + a_high * b_low + a_low * b_high) + a_low * b_low


def summed(received):
    zero = jnp.zeros((8, LANES), F32)
    chains = 4
    sums, errors = [zero] * chains, [zero] * chains
    for index in range(received.shape[0]):
        chain = index % chains
        sums[chain], error = two_sum(sums[chain], received[index])
        errors[chain] = errors[chain] + error
    total, rest = sums[0], errors[0]
    for chain in range(1, chains):
        total, error = two_sum(total, sums[chain])
        rest = rest + errors[chain] + error
    total, error = two_sum(total, pltpu.roll(total, 4, 0))
    return total, rest + pltpu.roll(rest, 4, 0) + error


def sum_kernel(received, message):
    total, rest = summed(received)
    total = total + jnp.where(lane_ids() % 32 < PROBES, 0.0, roll_lanes(rest, PROBES))
    message[...] = jnp.broadcast_to(total[None, 0:4], message.shape)


def factor_kernel(count, received, image, basis, factor):
    upper_half = lax.broadcasted_iota(jnp.int32, (8, LANES), 0) < 4
    total, rest = summed(received)
    rest = rest + roll_lanes(total, -PROBES)

    def unpack(value):
        low = jnp.where(upper_half, value, roll_lanes(value, -32))
        high = jnp.where(upper_half, roll_lanes(value, -64), roll_lanes(value, -96))
        return jnp.concatenate([low, high], axis=0)

    high, low = two_sum(unpack(total), unpack(rest))

    shape = (PROBES, LANES)
    wide = lax.broadcasted_iota(jnp.int32, shape, 1)
    rows = lax.broadcasted_iota(jnp.int32, shape, 0)
    high = jnp.where(wide < PROBES, high, jnp.where(wide == rows + PROBES, 1.0, 0.0))
    low = jnp.where(wide < PROBES, low, 0.0)
    for step in range(PROBES - 1):
        row_high = jnp.broadcast_to(high[step : step + 1], shape)
        row_low = jnp.broadcast_to(low[step : step + 1], shape)
        column_high = jnp.broadcast_to(high[:, step : step + 1], shape)
        column_low = jnp.broadcast_to(low[:, step : step + 1], shape)
        pivot_high = jnp.broadcast_to(row_high[:, step : step + 1], shape)
        pivot_low = jnp.broadcast_to(row_low[:, step : step + 1], shape)
        inverse = 1.0 / pivot_high
        ratio = jnp.where(rows > step, column_high * inverse, 0.0)
        ratio_parts = split(ratio)
        taken = ratio * pivot_high
        remainder = ((column_high - taken) - product_error(ratio_parts, split(pivot_high), taken)) + (
            column_low - ratio * pivot_low
        )
        ratio_low = jnp.where(rows > step, remainder * inverse, 0.0)
        taken = ratio * row_high
        taken_error = product_error(ratio_parts, split(row_high), taken)
        high, error = two_sum(high, -taken)
        low = low + error - taken_error - (ratio * row_low + ratio_low * row_high)
        high, low = two_sum(high, low)

    diagonal = jnp.sum(jnp.where(wide == rows, high, 0.0), axis=1, keepdims=True)
    root = jnp.broadcast_to(jnp.sqrt(diagonal), shape)
    size = math.sqrt(count)
    upper = high / root
    factor[...] = jnp.where(wide >= rows, upper * (1.0 / size), 0.0)[:, :PROBES]
    inverse = upper * size
    columns = [
        jnp.broadcast_to(inverse[:, PROBES + index : PROBES + index + 1], shape) for index in range(PROBES)
    ]

    def row(y, carry):
        for level in range(LEVELS):
            outs = [None, None]
            for index in range(PROBES):
                value = image[y, level, index // 8, pl.ds(index % 8, 1), :]
                for part in range(index // 8, 2):
                    term = columns[index][8 * part : 8 * part + 8] * value
                    outs[part] = term if outs[part] is None else outs[part] + term
            for part in range(2):
                basis[level, pl.ds(part * 8 * ROWS + y, 8, stride=ROWS), :] = outs[part]
        return carry

    lax.fori_loop(0, ROWS, row, 0, unroll=True)


def call(kernel, outs, scratch=(), inputs=pltpu.VMEM, grant=40):
    vmem = pl.BlockSpec(memory_space=pltpu.VMEM)

    def run(*operands):
        return pl.pallas_call(
            kernel,
            out_shape=[jax.ShapeDtypeStruct(shape, F32) for shape in outs],
            in_specs=[pl.BlockSpec(memory_space=inputs)] * len(operands),
            out_specs=[vmem] * len(outs),
            scratch_shapes=list(scratch),
            compiler_params=pltpu.CompilerParams(vmem_limit_bytes=grant << 20),
        )(*operands)

    return run


def body(probes, winds, diffusivity, mixing, prior_scale, obs_weight):
    tile = (8, LANES)
    size_x, size_y = lax.axis_size("gx"), lax.axis_size("gy")
    count = LEVELS * ROWS * LANES * size_x * size_y

    def shift(value, axis, step):
        number = lax.axis_size(axis)
        pairs = [(i, i + step) for i in range(number) if 0 <= i + step < number]
        return lax.ppermute(value, axis, pairs)

    def exchange(message, axis):
        received = lax.all_to_all(message, axis, 0, 0)
        return received.reshape((message.shape[0] // 2,) + tile)

    flat = (LEVELS, PROBES * ROWS, LANES)
    source, east, west, fields, prior = call(
        pack_kernel,
        [(ROWS, LEVELS, 2) + tile, (X_PARTS,) + tile, (X_PARTS,) + tile, (FIELDS, ROWS, LANES), (LEVELS, ROWS, LANES)],
        [pltpu.VMEM(flat, F32), pltpu.SemaphoreType.DMA((7,))],
        pltpu.HBM,
    )(*(pltpu.with_memory_space_constraint(a, pltpu.HBM) for a in (probes.reshape(flat), winds, diffusivity, mixing, prior_scale, obs_weight)))
    from_west = shift(east, "gx", 1)
    from_east = shift(west, "gx", -1)
    halo, north, south = call(
        merge_kernel, [(X_PARTS,) + tile, (Y_PARTS,) + tile, (Y_PARTS,) + tile]
    )(from_west, from_east, source, fields)
    from_south = shift(north, "gy", 1)
    from_north = shift(south, "gy", -1)
    field = (EXT, LEVELS, 3) + tile
    image, message = call(
        stencil_kernel,
        [(ROWS, LEVELS, 2) + tile, (size_x, 4, LANES)],
        [
            pltpu.VMEM(field, F32),
            pltpu.VMEM(field, F32),
            pltpu.VMEM(field, F32),
            pltpu.VMEM((STEPS - 1,) + field, F32),
            pltpu.VMEM((2, DERIVED, EXT, LANES), F32),
            pltpu.VMEM((ROWS, PROBES * SLICES, LEVELS * LANES), jnp.bfloat16),
        ],
    )(source, halo, fields, prior, from_south, from_north)
    received = exchange(message, "gx")
    (message,) = call(sum_kernel, [(size_y, 4, LANES)])(received)
    received = exchange(message, "gy")
    basis, factor = call(
        lambda *refs: factor_kernel(count, *refs),
        [flat, (PROBES, PROBES)],
    )(received, image)
    return basis.reshape(probes.shape), factor


def solution(mesh):
    placed = (
        P(None, None, "gy", "gx"),
        P(None, None, "gy", "gx"),
        P(None, "gy", "gx"),
        P("gy", "gx"),
        P(None, "gy", "gx"),
        P(None, "gy", "gx"),
    )
    return jax.shard_map(
        body,
        mesh=mesh,
        in_specs=placed,
        out_specs=(P(None, None, "gy", "gx"), P()),
        check_vma=False,
    )
```

```python
import math
import jax
import jax.numpy as jnp
from jax import lax
from jax.experimental import pallas as pl
from jax.experimental.pallas import tpu as pltpu
from jax.sharding import PartitionSpec as P

STEPS = 4
LEVELS = 4
PROBES = 16
HALO = 2 * STEPS
LANES = 128
ROWS = 16
EXT = ROWS + 2 * HALO
F32 = jnp.float32

FIELDS = 17
GROUPS = 3
EAST, WEST, NORTH, SOUTH, CENTER, RATE, OBS, DERIVED = 0, 4, 8, 12, 16, 20, 21, 25
X_PARTS = ROWS + 2 * GROUPS
Y_SOURCE, Y_HALO, Y_COEF, Y_COEF_HALO, Y_PARTS = 0, 64, 72, 89, 92
SLICES = 4


def lane_ids():
    return lax.broadcasted_iota(jnp.int32, (8, LANES), 1)


def roll_lanes(value, shift):
    shift = shift % LANES
    return value if shift == 0 else pltpu.roll(value, shift, value.ndim - 1)


def pack_kernel(
    probes_in, winds_in, diffusivity_in, mixing_in, prior_in, obs_in,
    source, east, west, fields, prior, probes, sems,
):
    coef_copies = [
        pltpu.make_async_copy(diffusivity_in, fields.at[pl.ds(0, 4)], sems.at[0]),
        pltpu.make_async_copy(winds_in.at[0], fields.at[pl.ds(4, 4)], sems.at[1]),
        pltpu.make_async_copy(winds_in.at[1], fields.at[pl.ds(8, 4)], sems.at[2]),
        pltpu.make_async_copy(obs_in, fields.at[pl.ds(12, 4)], sems.at[3]),
        pltpu.make_async_copy(mixing_in, fields.at[16], sems.at[4]),
    ]
    source_copies = [
        pltpu.make_async_copy(probes_in, probes, sems.at[5]),
        pltpu.make_async_copy(prior_in, prior, sems.at[6]),
    ]
    for copy in source_copies + coef_copies:
        copy.start()
    lanes = lane_ids()
    half = lanes // 8

    def put(held, value, slot):
        to_east, to_west = held
        to_east = jnp.where(half == 2 * slot + 1, roll_lanes(value, 16 * slot + 8 - (LANES - HALO)), to_east)
        to_west = jnp.where(half == 2 * slot, roll_lanes(value, 16 * slot), to_west)
        return to_east, to_west

    zero = jnp.zeros((8, LANES), F32)

    def row(y, carry):
        held = (zero, zero)
        for level in range(LEVELS):
            scale = prior[level, pl.ds(y, 1), :]
            for part in range(2):
                value = probes[level, pl.ds(part * 8 * ROWS + y, 8, stride=ROWS), :] * scale
                source[y, level, part] = value
                held = put(held, value, 2 * level + part)
        east[y], west[y] = held
        return carry

    for copy in coef_copies:
        copy.wait()
    for group in range(GROUPS):
        for tile in range(2):
            held = (zero, zero)
            for slot in range(8):
                field = 8 * group + slot
                if field < FIELDS:
                    held = put(held, fields[field, pl.ds(8 * tile, 8), :], slot)
            east[ROWS + 2 * group + tile], west[ROWS + 2 * group + tile] = held
    for copy in source_copies:
        copy.wait()
    lax.fori_loop(0, ROWS, row, 0, unroll=True)


def merge_kernel(from_west, from_east, source, fields, halo, north, south):
    inner = lane_ids() % 16 < 8
    for index in range(X_PARTS):
        halo[index] = jnp.where(inner, from_east[index], from_west[index])
    for tile, out in ((0, south), (1, north)):
        for y in range(8):
            for level in range(LEVELS):
                for part in range(2):
                    out[(y * LEVELS + level) * 2 + part] = source[8 * tile + y, level, part]
            out[Y_HALO + y] = jnp.where(inner, from_east[8 * tile + y], from_west[8 * tile + y])
        for field in range(FIELDS):
            out[Y_COEF + field] = fields[field, pl.ds(8 * tile, 8), :]
        for group in range(GROUPS):
            index = ROWS + 2 * group + tile
            out[Y_COEF_HALO + group] = jnp.where(inner, from_east[index], from_west[index])


def strip_of(lanes, first, second, halo_first, halo_second, slot_first, slot_second):
    value = roll_lanes(first, 24)
    value = jnp.where(lanes >= 24, roll_lanes(halo_first, 24 - 16 * slot_first), value)
    value = jnp.where(lanes >= 40, roll_lanes(first, 40), value)
    value = jnp.where(lanes >= 64, roll_lanes(second, 88), value)
    value = jnp.where(lanes >= 88, roll_lanes(halo_second, 88 - 16 * slot_second), value)
    return jnp.where(lanes >= 104, roll_lanes(second, 104), value)


def two_sum(a, b):
    total = a + b
    other = total - a
    return total, (a - (total - other)) + (b - other)


def derive(coefs, rows, kind, values):
    rate = values[16]
    coefs[kind, RATE, rows, :] = rate
    for level in range(LEVELS):
        kappa, wind_x, wind_y = values[level], values[4 + level], values[8 + level]
        coefs[kind, EAST + level, rows, :] = kappa - wind_x
        coefs[kind, WEST + level, rows, :] = kappa + wind_x
        coefs[kind, NORTH + level, rows, :] = kappa - wind_y
        coefs[kind, SOUTH + level, rows, :] = kappa + wind_y
        sides = 1.0 if level in (0, LEVELS - 1) else 2.0
        coefs[kind, CENTER + level, rows, :] = 1.0 - 4.0 * kappa - sides * rate
        coefs[kind, OBS + level, rows, :] = values[12 + level]


def derive_both(coefs, tile, main, packed):
    lanes = lane_ids()
    strips = [
        strip_of(lanes, main[field], main[field], packed[field // 8], packed[field // 8], field % 8, field % 8)
        for field in range(FIELDS)
    ]
    for kind, values in ((0, main), (1, strips)):
        derive(coefs, slice(8 * tile, 8 * tile + 8), kind, values)


def vertical(values, level):
    if level == 0:
        return values[1]
    if level == LEVELS - 1:
        return values[LEVELS - 2]
    return values[level - 1] + values[level + 1]


def forward(get, coef_of, low, high, parts, emit):
    def load(y):
        return [[get(y, level, part) for level in range(LEVELS)] for part in parts]

    before, center = load(low - 1), load(low)
    for y in range(low, high):
        after = load(y + 1)
        coef = lambda index: coef_of(parts[0] // 2, index, y)
        rate = coef(RATE)
        results = [[None] * LEVELS for part in parts]
        for level in range(LEVELS):
            middle, east, west, north, south = [coef(base + level) for base in (CENTER, EAST, WEST, NORTH, SOUTH)]
            for index in range(len(parts)):
                value = center[index][level]
                results[index][level] = (
                    (middle * value + rate * vertical(center[index], level))
                    + (north * after[index][level] + south * before[index][level])
                    + (east * roll_lanes(value, -1) + west * roll_lanes(value, 1))
                )
        emit(y, parts, results)
        before, center = center, after


def adjoint(get, coef_of, low, high, parts, emit):
    def load(y):
        return [[get(y, level, part) for level in range(LEVELS)] for part in parts]

    def taken(base, y, values):
        own = [coef_of(parts[0] // 2, base + level, y) for level in range(LEVELS)]
        return [[own[level] * row[level] for level in range(LEVELS)] for row in values]

    pushed = taken(NORTH, low - 1, load(low - 1))
    partial = None
    for y in range(low, high + 1):
        center = load(y)
        if partial is not None:
            pulled = taken(SOUTH, y, center)
            emit(y - 1, parts, [
                [partial[index][level] + pulled[index][level] for level in range(LEVELS)] for index in range(len(parts))
            ])
        if y == high:
            break
        coef = lambda index: coef_of(parts[0] // 2, index, y)
        rate = coef(RATE)
        partial = [[None] * LEVELS for part in parts]
        for level in range(LEVELS):
            middle, east, west = [coef(base + level) for base in (CENTER, EAST, WEST)]
            for index in range(len(parts)):
                value = center[index][level]
                partial[index][level] = (
                    (middle * value + rate * vertical(center[index], level))
                    + (roll_lanes(west * value, -1) + roll_lanes(east * value, 1))
                    + pushed[index][level]
                )
        pushed = taken(NORTH, y, center)


GROUPED = ((2,), (0, 1))


def advance(step, low, high, get, put, coef_of):
    def emit(y, parts, results):
        for index, part in enumerate(parts):
            for level in range(LEVELS):
                value = results[index][level]
                if step < STEPS:
                    value = value + get(0, y, level, part)
                elif step == STEPS:
                    value = value * coef_of(part // 2, OBS + level, y)
                put(step, y, level, part, value)

    before = lambda y, level, part: get(step - 1, y, level, part)
    for parts in GROUPED:
        (forward if step <= STEPS else adjoint)(before, coef_of, low, high, parts, emit)


def inner_kernel(source, halo, fields, inner, coefs):
    lanes = lane_ids()
    for tile in range(2):
        main = [fields[field, 8 * tile : 8 * tile + 8, :] for field in range(FIELDS)]
        derive_both(coefs, tile, main, [halo[ROWS + 2 * group + tile] for group in range(GROUPS)])
    for y in range(ROWS):
        packed = halo[y]
        for level in range(LEVELS):
            low, high = source[y, level, 0], source[y, level, 1]
            inner[0, y, level, 0] = low
            inner[0, y, level, 1] = high
            inner[0, y, level, 2] = strip_of(lanes, low, high, packed, packed, 2 * level, 2 * level + 1)

    def get(step, y, level, part):
        return inner[step, y - HALO, level, part]

    def put(step, y, level, part, value):
        inner[step, y - HALO, level, part] = value

    def coef_of(kind, index, y):
        return coefs[kind, index, y - HALO : y - HALO + 1, :]

    for step in range(1, HALO):
        advance(step, HALO + step, HALO + ROWS - step, get, put, coef_of)


def stencil_kernel(inner, coefs, prior, from_south, from_north, image, message, outer, outer_coefs, slices):
    lanes = lane_ids()
    for tile, ref in ((0, from_south), (1, from_north)):
        main = [ref[Y_COEF + field] for field in range(FIELDS)]
        derive_both(outer_coefs, tile, main, [ref[Y_COEF_HALO + group] for group in range(GROUPS)])
        for y in range(HALO):
            packed = ref[Y_HALO + y]
            for level in range(LEVELS):
                low, high = ref[(y * LEVELS + level) * 2], ref[(y * LEVELS + level) * 2 + 1]
                outer[0, HALO * tile + y, level, 0] = low
                outer[0, HALO * tile + y, level, 1] = high
                outer[0, HALO * tile + y, level, 2] = strip_of(lanes, low, high, packed, packed, 2 * level, 2 * level + 1)

    def place(step, y):
        if y < HALO + step:
            return outer, y - step
        if y >= HALO + ROWS - step:
            return outer, HALO + y - (HALO + ROWS - step)
        return inner, y - HALO

    def get(step, y, level, part):
        ref, row = place(step, y)
        return ref[step, row, level, part]

    def put(step, y, level, part, value):
        ref, row = place(step, y)
        ref[step, row, level, part] = value

    def coef_of(kind, index, y):
        if y < HALO:
            return outer_coefs[kind, index, y : y + 1, :]
        if y >= HALO + ROWS:
            return outer_coefs[kind, index, y - ROWS : y - ROWS + 1, :]
        return coefs[kind, index, y - HALO : y - HALO + 1, :]

    for step in range(1, HALO):
        advance(step, step, step + HALO, get, put, coef_of)
        advance(step, EXT - HALO - step, EXT - step, get, put, coef_of)

    zero = jnp.zeros((8, LANES), F32)
    most = [zero, zero]

    def total_of(y, part, level, value):
        first, second, third = [get(step, y, level, part) for step in range(STEPS + 1, 2 * STEPS)]
        return (first + second) + (third + value)

    def emit_last(y, parts, results):
        for level in range(LEVELS):
            if parts == (2,):
                outer[2 * STEPS, y - HALO, level, 2] = total_of(y, 2, level, results[0][level])
                continue
            scale = prior[level, y - HALO : y - HALO + 1, :]
            strip = outer[2 * STEPS, y - HALO, level, 2]
            for part in parts:
                value = total_of(y, part, level, results[part][level])
                value = jnp.where(lanes < HALO, roll_lanes(strip, -40 - 64 * part), value)
                value = jnp.where(lanes >= LANES - HALO, roll_lanes(strip, 104 - 64 * part), value)
                value = value * scale
                image[y - HALO, level, part] = value
                most[part] = jnp.maximum(most[part], jnp.abs(value))

    for parts in GROUPED:
        adjoint(lambda y, level, part: get(2 * STEPS - 1, y, level, part), coef_of, HALO, HALO + ROWS, parts, emit_last)

    magics = []
    for part in range(2):
        top = jnp.broadcast_to(jnp.max(most[part], axis=1, keepdims=True), (8, LANES))
        scaled = top * (2.0**23 + 1.0)
        power = jnp.abs(scaled - scaled * (1.0 - 2.0**-24))
        magics.append([power * (1.5 * 2.0 ** (23 - 6 - 8 * index)) for index in range(SLICES)])

    def slice_row(y, carry):
        for level in range(LEVELS):
            pieces = []
            for part in range(2):
                rest = image[y, level, part]
                own = []
                for index in range(SLICES):
                    magic = magics[part][index]
                    piece = (rest + magic) - magic
                    rest = rest - piece
                    own.append(piece)
                pieces.append(own)
            for index in range(SLICES):
                both = jnp.concatenate([pieces[0][index], pieces[1][index]], axis=0)
                slices[y, pl.ds(PROBES * index, PROBES), pl.ds(LANES * level, LANES)] = both.astype(jnp.bfloat16)
        return carry

    lax.fori_loop(0, ROWS, slice_row, 0, unroll=True)

    width = PROBES * SLICES
    high = jnp.zeros((width, width), F32)
    low = jnp.zeros((width, width), F32)
    for pair in range(ROWS // 2):
        block = jnp.concatenate([slices[2 * pair], slices[2 * pair + 1]], axis=1)
        product = lax.dot_general(block, block, (((1,), (1,)), ((), ())), preferred_element_type=F32)
        high, error = two_sum(high, product)
        low = low + error

    def fold(high, low, blocks):
        total_high, total_low = None, None
        for block_high, block_low in blocks(high, low):
            if total_high is None:
                total_high, total_low = block_high, block_low
            else:
                total_high, error = two_sum(total_high, block_high)
                total_low = total_low + block_low + error
        return total_high, total_low

    def row_blocks(high, low):
        for index in range(SLICES):
            rows = slice(PROBES * index, PROBES * (index + 1))
            yield high[rows], low[rows]

    def lane_blocks(high, low):
        for index in range(SLICES):
            yield roll_lanes(high, -PROBES * index), roll_lanes(low, -PROBES * index)

    high, low = fold(high, low, row_blocks)
    rest = jnp.zeros((PROBES, LANES - width), F32)
    high, low = jnp.concatenate([high, rest], axis=1), jnp.concatenate([low, rest], axis=1)
    high, low = fold(high, low, lane_blocks)
    high, low = two_sum(high, low)

    wide = lax.broadcasted_iota(jnp.int32, (PROBES, LANES), 1)
    both = jnp.where(wide < PROBES, high, roll_lanes(low, PROBES))
    packed = both[0:8]
    for index in range(1, 4):
        value = both[8 * (index // 2) : 8 * (index // 2) + 8]
        if index % 2:
            value = pltpu.roll(value, 4, 0)
        packed = jnp.where(lanes // 32 == index, roll_lanes(value, 32 * index), packed)
    message[...] = jnp.broadcast_to(packed[None, 0:4], message.shape)


def split(a):
    scaled = a * 4097.0
    high = scaled - (scaled - a)
    return high, a - high


def product_error(a, b, product):
    a_high, a_low = a
    b_high, b_low = b
    return ((a_high * b_high - product) + a_high * b_low + a_low * b_high) + a_low * b_low


def summed(received):
    zero = jnp.zeros((8, LANES), F32)
    chains = 4
    sums, errors = [zero] * chains, [zero] * chains
    for index in range(received.shape[0]):
        chain = index % chains
        sums[chain], error = two_sum(sums[chain], received[index])
        errors[chain] = errors[chain] + error
    total, rest = sums[0], errors[0]
    for chain in range(1, chains):
        total, error = two_sum(total, sums[chain])
        rest = rest + errors[chain] + error
    total, error = two_sum(total, pltpu.roll(total, 4, 0))
    return total, rest + pltpu.roll(rest, 4, 0) + error


def sum_kernel(received, message):
    total, rest = summed(received)
    total = total + jnp.where(lane_ids() % 32 < PROBES, 0.0, roll_lanes(rest, PROBES))
    message[...] = jnp.broadcast_to(total[None, 0:4], message.shape)


def factor_kernel(count, received, image, basis, factor, held, sems):
    upper_half = lax.broadcasted_iota(jnp.int32, (8, LANES), 0) < 4
    total, rest = summed(received)
    rest = rest + roll_lanes(total, -PROBES)

    def unpack(value):
        low = jnp.where(upper_half, value, roll_lanes(value, -32))
        high = jnp.where(upper_half, roll_lanes(value, -64), roll_lanes(value, -96))
        return jnp.concatenate([low, high], axis=0)

    high, low = two_sum(unpack(total), unpack(rest))

    shape = (PROBES, LANES)
    wide = lax.broadcasted_iota(jnp.int32, shape, 1)
    rows = lax.broadcasted_iota(jnp.int32, shape, 0)
    high = jnp.where(wide < PROBES, high, jnp.where(wide == rows + PROBES, 1.0, 0.0))
    low = jnp.where(wide < PROBES, low, 0.0)

    def column(index):
        return [jnp.broadcast_to(value[:, index : index + 1], shape) for value in (high, low)]

    def row_of(value, index):
        return jnp.broadcast_to(value[index : index + 1], shape)

    own_high, own_low = column(0)
    for step in range(PROBES - 1):
        next_high, next_low = column(step + 1)
        pivot_high, pivot_low = row_of(own_high, step), row_of(own_low, step)
        inverse = 1.0 / pivot_high
        ratio = jnp.where(rows > step, own_high * inverse, 0.0)
        ratio_parts = split(ratio)
        taken = ratio * pivot_high
        remainder = ((own_high - taken) - product_error(ratio_parts, split(pivot_high), taken)) + (
            own_low - ratio * pivot_low
        )
        ratio_low = jnp.where(rows > step, remainder * inverse, 0.0)

        def reduce(high, low):
            row_high, row_low = row_of(high, step), row_of(low, step)
            taken = ratio * row_high
            error_taken = product_error(ratio_parts, split(row_high), taken)
            high, error = two_sum(high, -taken)
            low = low + error - error_taken - (ratio * row_low + ratio_low * row_high)
            return two_sum(high, low)

        own_high, own_low = reduce(next_high, next_low)
        high, low = reduce(high, low)

    diagonal = jnp.sum(jnp.where(wide == rows, high, 0.0), axis=1, keepdims=True)
    root = jnp.broadcast_to(jnp.sqrt(diagonal), shape)
    size = math.sqrt(count)
    upper = high / root
    factor[...] = jnp.where(wide >= rows, upper * (1.0 / size), 0.0)[:, :PROBES]
    inverse = upper * size
    columns = [
        jnp.broadcast_to(inverse[:, PROBES + index : PROBES + index + 1], shape) for index in range(PROBES)
    ]

    copies = []
    for level in range(LEVELS):
        for y in range(ROWS):
            outs = [None, None]
            for index in range(PROBES):
                value = image[y, level, index // 8, index % 8 : index % 8 + 1, :]
                for part in range(index // 8, 2):
                    term = columns[index][8 * part : 8 * part + 8] * value
                    outs[part] = term if outs[part] is None else outs[part] + term
            for part in range(2):
                held[level, pl.ds(part * 8 * ROWS + y, 8, stride=ROWS), :] = outs[part]
        copies.append(pltpu.make_async_copy(held.at[level], basis.at[level], sems.at[level]))
        copies[-1].start()
    for copy in copies:
        copy.wait()


def call(kernel, outs, scratch=(), inputs=pltpu.VMEM, spaces=None, cost=None):
    def run(*operands):
        return pl.pallas_call(
            kernel,
            out_shape=[jax.ShapeDtypeStruct(shape, F32) for shape in outs],
            in_specs=[pl.BlockSpec(memory_space=inputs)] * len(operands),
            out_specs=[pl.BlockSpec(memory_space=space) for space in spaces or [pltpu.VMEM] * len(outs)],
            scratch_shapes=list(scratch),
            cost_estimate=cost,
            compiler_params=pltpu.CompilerParams(vmem_limit_bytes=40 << 20),
        )(*operands)

    return run


def body(probes, winds, diffusivity, mixing, prior_scale, obs_weight):
    tile = (8, LANES)
    size_x, size_y = lax.axis_size("gx"), lax.axis_size("gy")
    count = LEVELS * ROWS * LANES * size_x * size_y

    def shift(value, axis, step):
        number = lax.axis_size(axis)
        pairs = [(i, i + step) for i in range(number) if 0 <= i + step < number]
        return lax.ppermute(value, axis, pairs)

    def exchange(message, axis):
        received = lax.all_to_all(message, axis, 0, 0)
        return received.reshape((message.shape[0] // 2,) + tile)

    flat = (LEVELS, PROBES * ROWS, LANES)
    source, east, west, fields, prior = call(
        pack_kernel,
        [(ROWS, LEVELS, 2) + tile, (X_PARTS,) + tile, (X_PARTS,) + tile, (FIELDS, ROWS, LANES), (LEVELS, ROWS, LANES)],
        [pltpu.VMEM(flat, F32), pltpu.SemaphoreType.DMA((7,))],
        pltpu.HBM,
    )(*(pltpu.with_memory_space_constraint(a, pltpu.HBM) for a in (probes.reshape(flat), winds, diffusivity, mixing, prior_scale, obs_weight)))
    from_west = shift(east, "gx", 1)
    from_east = shift(west, "gx", -1)
    halo, north, south = call(
        merge_kernel, [(X_PARTS,) + tile, (Y_PARTS,) + tile, (Y_PARTS,) + tile]
    )(from_west, from_east, source, fields)
    from_south = shift(north, "gy", 1)
    from_north = shift(south, "gy", -1)
    field = (ROWS, LEVELS, 3) + tile
    derived = (2, DERIVED, ROWS, LANES)
    values = HALO * math.prod(field)
    inner, coefs = call(
        inner_kernel,
        [(HALO,) + field, derived],
        cost=pl.CostEstimate(flops=20 * values, bytes_accessed=8 * values, transcendentals=0),
    )(source, halo, fields)
    image, message = call(
        stencil_kernel,
        [(ROWS, LEVELS, 2) + tile, (size_x, 4, LANES)],
        [
            pltpu.VMEM((HALO + 1,) + field, F32),
            pltpu.VMEM(derived, F32),
            pltpu.VMEM((ROWS, PROBES * SLICES, LEVELS * LANES), jnp.bfloat16),
        ],
    )(inner, coefs, prior, from_south, from_north)
    received = exchange(message, "gx")
    (message,) = call(sum_kernel, [(size_y, 4, LANES)])(received)
    received = exchange(message, "gy")
    basis, factor = call(
        lambda *refs: factor_kernel(count, *refs),
        [flat, (PROBES, PROBES)],
        [pltpu.VMEM(flat, F32), pltpu.SemaphoreType.DMA((LEVELS,))],
        spaces=[pltpu.HBM, pltpu.VMEM],
    )(received, image)
    return basis.reshape(probes.shape), factor


def solution(mesh):
    placed = (
        P(None, None, "gy", "gx"),
        P(None, None, "gy", "gx"),
        P(None, "gy", "gx"),
        P("gy", "gx"),
        P(None, "gy", "gx"),
        P(None, "gy", "gx"),
    )
    return jax.shard_map(
        body,
        mesh=mesh,
        in_specs=placed,
        out_specs=(P(None, None, "gy", "gx"), P()),
        check_vma=False,
    )
```

```python
import math
import jax
import jax.numpy as jnp
from jax import lax
from jax.experimental import pallas as pl
from jax.experimental.pallas import tpu as pltpu
from jax.sharding import PartitionSpec as P

STEPS = 4
LEVELS = 4
PROBES = 16
HALO = 2 * STEPS
LANES = 128
ROWS = 16
EXT = ROWS + 2 * HALO
F32 = jnp.float32

FIELDS = 17
GROUPS = 3
EAST, WEST, NORTH, SOUTH, CENTER, RATE, OBS, DERIVED = 0, 4, 8, 12, 16, 20, 21, 25
X_PARTS = ROWS + 2 * GROUPS
Y_SOURCE, Y_HALO, Y_COEF, Y_COEF_HALO, Y_PARTS = 0, 64, 72, 89, 92
SLICES = 4


def lane_ids():
    return lax.broadcasted_iota(jnp.int32, (8, LANES), 1)


def roll_lanes(value, shift):
    shift = shift % LANES
    return value if shift == 0 else pltpu.roll(value, shift, value.ndim - 1)


def pack_kernel(
    probes_in, winds_in, diffusivity_in, mixing_in, prior_in, obs_in,
    source, east, west, fields, prior, probes, sems,
):
    coef_copies = [
        pltpu.make_async_copy(diffusivity_in, fields.at[pl.ds(0, 4)], sems.at[0]),
        pltpu.make_async_copy(winds_in.at[0], fields.at[pl.ds(4, 4)], sems.at[1]),
        pltpu.make_async_copy(winds_in.at[1], fields.at[pl.ds(8, 4)], sems.at[2]),
        pltpu.make_async_copy(obs_in, fields.at[pl.ds(12, 4)], sems.at[3]),
        pltpu.make_async_copy(mixing_in, fields.at[16], sems.at[4]),
    ]
    source_copies = [
        pltpu.make_async_copy(probes_in, probes, sems.at[5]),
        pltpu.make_async_copy(prior_in, prior, sems.at[6]),
    ]
    for copy in source_copies + coef_copies:
        copy.start()
    lanes = lane_ids()
    half = lanes // 8

    def put(held, value, slot):
        to_east, to_west = held
        to_east = jnp.where(half == 2 * slot + 1, roll_lanes(value, 16 * slot + 8 - (LANES - HALO)), to_east)
        to_west = jnp.where(half == 2 * slot, roll_lanes(value, 16 * slot), to_west)
        return to_east, to_west

    zero = jnp.zeros((8, LANES), F32)

    def row(y, carry):
        held = (zero, zero)
        for level in range(LEVELS):
            scale = prior[level, pl.ds(y, 1), :]
            for part in range(2):
                value = probes[level, pl.ds(part * 8 * ROWS + y, 8, stride=ROWS), :] * scale
                source[y, level, part] = value
                held = put(held, value, 2 * level + part)
        east[y], west[y] = held
        return carry

    for copy in coef_copies:
        copy.wait()
    for group in range(GROUPS):
        for tile in range(2):
            held = (zero, zero)
            for slot in range(8):
                field = 8 * group + slot
                if field < FIELDS:
                    held = put(held, fields[field, pl.ds(8 * tile, 8), :], slot)
            east[ROWS + 2 * group + tile], west[ROWS + 2 * group + tile] = held
    for copy in source_copies:
        copy.wait()
    lax.fori_loop(0, ROWS, row, 0, unroll=True)


def merge_kernel(from_west, from_east, source, fields, halo, north, south):
    inner = lane_ids() % 16 < 8
    for index in range(X_PARTS):
        halo[index] = jnp.where(inner, from_east[index], from_west[index])
    for tile, out in ((0, south), (1, north)):
        for y in range(8):
            for level in range(LEVELS):
                for part in range(2):
                    out[(y * LEVELS + level) * 2 + part] = source[8 * tile + y, level, part]
            out[Y_HALO + y] = jnp.where(inner, from_east[8 * tile + y], from_west[8 * tile + y])
        for field in range(FIELDS):
            out[Y_COEF + field] = fields[field, pl.ds(8 * tile, 8), :]
        for group in range(GROUPS):
            index = ROWS + 2 * group + tile
            out[Y_COEF_HALO + group] = jnp.where(inner, from_east[index], from_west[index])


def strip_of(lanes, first, second, halo_first, halo_second, slot_first, slot_second):
    value = roll_lanes(first, 24)
    value = jnp.where(lanes >= 24, roll_lanes(halo_first, 24 - 16 * slot_first), value)
    value = jnp.where(lanes >= 40, roll_lanes(first, 40), value)
    value = jnp.where(lanes >= 64, roll_lanes(second, 88), value)
    value = jnp.where(lanes >= 88, roll_lanes(halo_second, 88 - 16 * slot_second), value)
    return jnp.where(lanes >= 104, roll_lanes(second, 104), value)


def two_sum(a, b):
    total = a + b
    other = total - a
    return total, (a - (total - other)) + (b - other)


def derive(coefs, rows, kind, values):
    rate = values[16]
    coefs[kind, RATE, rows, :] = rate
    for level in range(LEVELS):
        kappa, wind_x, wind_y = values[level], values[4 + level], values[8 + level]
        coefs[kind, EAST + level, rows, :] = kappa - wind_x
        coefs[kind, WEST + level, rows, :] = kappa + wind_x
        coefs[kind, NORTH + level, rows, :] = kappa - wind_y
        coefs[kind, SOUTH + level, rows, :] = kappa + wind_y
        sides = 1.0 if level in (0, LEVELS - 1) else 2.0
        coefs[kind, CENTER + level, rows, :] = 1.0 - 4.0 * kappa - sides * rate
        coefs[kind, OBS + level, rows, :] = values[12 + level]


def derive_both(coefs, tile, main, packed):
    lanes = lane_ids()
    strips = [
        strip_of(lanes, main[field], main[field], packed[field // 8], packed[field // 8], field % 8, field % 8)
        for field in range(FIELDS)
    ]
    for kind, values in ((0, main), (1, strips)):
        derive(coefs, slice(8 * tile, 8 * tile + 8), kind, values)


def vertical(values, level):
    if level == 0:
        return values[1]
    if level == LEVELS - 1:
        return values[LEVELS - 2]
    return values[level - 1] + values[level + 1]


def forward(get, coef_of, low, high, parts, emit):
    def load(y):
        return [[get(y, level, part) for level in range(LEVELS)] for part in parts]

    before, center = load(low - 1), load(low)
    for y in range(low, high):
        after = load(y + 1)
        coef = lambda index: coef_of(parts[0] // 2, index, y)
        rate = coef(RATE)
        results = [[None] * LEVELS for part in parts]
        for level in range(LEVELS):
            middle, east, west, north, south = [coef(base + level) for base in (CENTER, EAST, WEST, NORTH, SOUTH)]
            for index in range(len(parts)):
                value = center[index][level]
                results[index][level] = (
                    (middle * value + rate * vertical(center[index], level))
                    + (north * after[index][level] + south * before[index][level])
                    + (east * roll_lanes(value, -1) + west * roll_lanes(value, 1))
                )
        emit(y, parts, results)
        before, center = center, after


def adjoint(get, coef_of, low, high, parts, emit):
    def load(y):
        return [[get(y, level, part) for level in range(LEVELS)] for part in parts]

    def taken(base, y, values):
        own = [coef_of(parts[0] // 2, base + level, y) for level in range(LEVELS)]
        return [[own[level] * row[level] for level in range(LEVELS)] for row in values]

    pushed = taken(NORTH, low - 1, load(low - 1))
    partial = None
    for y in range(low, high + 1):
        center = load(y)
        if partial is not None:
            pulled = taken(SOUTH, y, center)
            emit(y - 1, parts, [
                [partial[index][level] + pulled[index][level] for level in range(LEVELS)] for index in range(len(parts))
            ])
        if y == high:
            break
        coef = lambda index: coef_of(parts[0] // 2, index, y)
        rate = coef(RATE)
        partial = [[None] * LEVELS for part in parts]
        for level in range(LEVELS):
            middle, east, west = [coef(base + level) for base in (CENTER, EAST, WEST)]
            for index in range(len(parts)):
                value = center[index][level]
                partial[index][level] = (
                    (middle * value + rate * vertical(center[index], level))
                    + (roll_lanes(west * value, -1) + roll_lanes(east * value, 1))
                    + pushed[index][level]
                )
        pushed = taken(NORTH, y, center)


GROUPED = ((2,), (0, 1))


def advance(step, low, high, get, put, coef_of):
    def emit(y, parts, results):
        for index, part in enumerate(parts):
            for level in range(LEVELS):
                value = results[index][level]
                if step < STEPS:
                    value = value + get(0, y, level, part)
                elif step == STEPS:
                    value = value * coef_of(part // 2, OBS + level, y)
                put(step, y, level, part, value)

    before = lambda y, level, part: get(step - 1, y, level, part)
    for parts in GROUPED:
        (forward if step <= STEPS else adjoint)(before, coef_of, low, high, parts, emit)


def inner_kernel(source, halo, fields, inner, coefs):
    lanes = lane_ids()
    for tile in range(2):
        main = [fields[field, 8 * tile : 8 * tile + 8, :] for field in range(FIELDS)]
        derive_both(coefs, tile, main, [halo[ROWS + 2 * group + tile] for group in range(GROUPS)])
    for y in range(ROWS):
        packed = halo[y]
        for level in range(LEVELS):
            low, high = source[y, level, 0], source[y, level, 1]
            inner[0, y, level, 0] = low
            inner[0, y, level, 1] = high
            inner[0, y, level, 2] = strip_of(lanes, low, high, packed, packed, 2 * level, 2 * level + 1)

    def get(step, y, level, part):
        return inner[step, y - HALO, level, part]

    def put(step, y, level, part, value):
        inner[step, y - HALO, level, part] = value

    def coef_of(kind, index, y):
        return coefs[kind, index, y - HALO : y - HALO + 1, :]

    for step in range(1, HALO):
        advance(step, HALO + step, HALO + ROWS - step, get, put, coef_of)


def stencil_kernel(inner, coefs, prior, from_south, from_north, image, message, outer, outer_coefs, slices):
    lanes = lane_ids()
    for tile, ref in ((0, from_south), (1, from_north)):
        main = [ref[Y_COEF + field] for field in range(FIELDS)]
        derive_both(outer_coefs, tile, main, [ref[Y_COEF_HALO + group] for group in range(GROUPS)])
        for y in range(HALO):
            packed = ref[Y_HALO + y]
            for level in range(LEVELS):
                low, high = ref[(y * LEVELS + level) * 2], ref[(y * LEVELS + level) * 2 + 1]
                outer[0, HALO * tile + y, level, 0] = low
                outer[0, HALO * tile + y, level, 1] = high
                outer[0, HALO * tile + y, level, 2] = strip_of(lanes, low, high, packed, packed, 2 * level, 2 * level + 1)

    def place(step, y):
        if y < HALO + step:
            return outer, y - step
        if y >= HALO + ROWS - step:
            return outer, HALO + y - (HALO + ROWS - step)
        return inner, y - HALO

    def get(step, y, level, part):
        ref, row = place(step, y)
        return ref[step, row, level, part]

    def put(step, y, level, part, value):
        ref, row = place(step, y)
        ref[step, row, level, part] = value

    def coef_of(kind, index, y):
        if y < HALO:
            return outer_coefs[kind, index, y : y + 1, :]
        if y >= HALO + ROWS:
            return outer_coefs[kind, index, y - ROWS : y - ROWS + 1, :]
        return coefs[kind, index, y - HALO : y - HALO + 1, :]

    for step in range(1, HALO):
        advance(step, step, step + HALO, get, put, coef_of)
        advance(step, EXT - HALO - step, EXT - step, get, put, coef_of)

    zero = jnp.zeros((8, LANES), F32)
    most = [zero, zero]

    def total_of(y, part, level, value):
        first, second, third = [get(step, y, level, part) for step in range(STEPS + 1, 2 * STEPS)]
        return (first + second) + (third + value)

    def emit_last(y, parts, results):
        for level in range(LEVELS):
            if parts == (2,):
                outer[2 * STEPS, y - HALO, level, 2] = total_of(y, 2, level, results[0][level])
                continue
            scale = prior[level, y - HALO : y - HALO + 1, :]
            strip = outer[2 * STEPS, y - HALO, level, 2]
            for part in parts:
                value = total_of(y, part, level, results[part][level])
                value = jnp.where(lanes < HALO, roll_lanes(strip, -40 - 64 * part), value)
                value = jnp.where(lanes >= LANES - HALO, roll_lanes(strip, 104 - 64 * part), value)
                value = value * scale
                image[y - HALO, level, part] = value
                most[part] = jnp.maximum(most[part], jnp.abs(value))

    for parts in GROUPED:
        adjoint(lambda y, level, part: get(2 * STEPS - 1, y, level, part), coef_of, HALO, HALO + ROWS, parts, emit_last)

    magics = []
    for part in range(2):
        top = jnp.broadcast_to(jnp.max(most[part], axis=1, keepdims=True), (8, LANES))
        scaled = top * (2.0**23 + 1.0)
        power = jnp.abs(scaled - scaled * (1.0 - 2.0**-24))
        magics.append([power * (1.5 * 2.0 ** (23 - 6 - 8 * index)) for index in range(SLICES)])

    def slice_row(y, carry):
        for level in range(LEVELS):
            pieces = []
            for part in range(2):
                rest = image[y, level, part]
                own = []
                for index in range(SLICES):
                    magic = magics[part][index]
                    piece = (rest + magic) - magic
                    rest = rest - piece
                    own.append(piece)
                pieces.append(own)
            for index in range(SLICES):
                both = jnp.concatenate([pieces[0][index], pieces[1][index]], axis=0)
                slices[y, pl.ds(PROBES * index, PROBES), pl.ds(LANES * level, LANES)] = both.astype(jnp.bfloat16)
        return carry

    lax.fori_loop(0, ROWS, slice_row, 0, unroll=True)

    width = PROBES * SLICES
    high = jnp.zeros((width, width), F32)
    low = jnp.zeros((width, width), F32)
    for pair in range(ROWS // 2):
        block = jnp.concatenate([slices[2 * pair], slices[2 * pair + 1]], axis=1)
        product = lax.dot_general(block, block, (((1,), (1,)), ((), ())), preferred_element_type=F32)
        high, error = two_sum(high, product)
        low = low + error

    def fold(high, low, blocks):
        total_high, total_low = None, None
        for block_high, block_low in blocks(high, low):
            if total_high is None:
                total_high, total_low = block_high, block_low
            else:
                total_high, error = two_sum(total_high, block_high)
                total_low = total_low + block_low + error
        return total_high, total_low

    def row_blocks(high, low):
        for index in range(SLICES):
            rows = slice(PROBES * index, PROBES * (index + 1))
            yield high[rows], low[rows]

    def lane_blocks(high, low):
        for index in range(SLICES):
            yield roll_lanes(high, -PROBES * index), roll_lanes(low, -PROBES * index)

    high, low = fold(high, low, row_blocks)
    rest = jnp.zeros((PROBES, LANES - width), F32)
    high, low = jnp.concatenate([high, rest], axis=1), jnp.concatenate([low, rest], axis=1)
    high, low = fold(high, low, lane_blocks)
    high, low = two_sum(high, low)

    wide = lax.broadcasted_iota(jnp.int32, (PROBES, LANES), 1)
    both = jnp.where(wide < PROBES, high, roll_lanes(low, PROBES))
    packed = both[0:8]
    for index in range(1, 4):
        value = both[8 * (index // 2) : 8 * (index // 2) + 8]
        if index % 2:
            value = pltpu.roll(value, 4, 0)
        packed = jnp.where(lanes // 32 == index, roll_lanes(value, 32 * index), packed)
    message[...] = jnp.broadcast_to(packed[None, 0:4], message.shape)


def split(a):
    scaled = a * 4097.0
    high = scaled - (scaled - a)
    return high, a - high


def product_error(a, b, product):
    a_high, a_low = a
    b_high, b_low = b
    return ((a_high * b_high - product) + a_high * b_low + a_low * b_high) + a_low * b_low


def summed(received):
    zero = jnp.zeros((8, LANES), F32)
    chains = 4
    sums, errors = [zero] * chains, [zero] * chains
    for index in range(received.shape[0]):
        chain = index % chains
        sums[chain], error = two_sum(sums[chain], received[index])
        errors[chain] = errors[chain] + error
    total, rest = sums[0], errors[0]
    for chain in range(1, chains):
        total, error = two_sum(total, sums[chain])
        rest = rest + errors[chain] + error
    total, error = two_sum(total, pltpu.roll(total, 4, 0))
    return total, rest + pltpu.roll(rest, 4, 0) + error


def sum_kernel(received, message):
    total, rest = summed(received)
    total = total + jnp.where(lane_ids() % 32 < PROBES, 0.0, roll_lanes(rest, PROBES))
    message[...] = jnp.broadcast_to(total[None, 0:4], message.shape)


def factor_kernel(count, received, image, basis, factor, held, sems):
    upper_half = lax.broadcasted_iota(jnp.int32, (8, LANES), 0) < 4
    total, rest = summed(received)
    rest = rest + roll_lanes(total, -PROBES)

    def unpack(value):
        low = jnp.where(upper_half, value, roll_lanes(value, -32))
        high = jnp.where(upper_half, roll_lanes(value, -64), roll_lanes(value, -96))
        return jnp.concatenate([low, high], axis=0)

    high, low = two_sum(unpack(total), unpack(rest))

    shape = (PROBES, LANES)
    wide = lax.broadcasted_iota(jnp.int32, shape, 1)
    rows = lax.broadcasted_iota(jnp.int32, shape, 0)
    high = jnp.where(wide < PROBES, high, jnp.where(wide == rows + PROBES, 1.0, 0.0))
    low = jnp.where(wide < PROBES, low, 0.0)

    def column(index):
        return [jnp.broadcast_to(value[:, index : index + 1], shape) for value in (high, low)]

    def row_of(value, index):
        return jnp.broadcast_to(value[index : index + 1], shape)

    own_high, own_low = column(0)
    for step in range(PROBES - 1):
        next_high, next_low = column(step + 1)
        pivot_high, pivot_low = row_of(own_high, step), row_of(own_low, step)
        inverse = 1.0 / pivot_high
        ratio = jnp.where(rows > step, own_high * inverse, 0.0)
        ratio_parts = split(ratio)
        taken = ratio * pivot_high
        remainder = ((own_high - taken) - product_error(ratio_parts, split(pivot_high), taken)) + (
            own_low - ratio * pivot_low
        )
        ratio_low = jnp.where(rows > step, remainder * inverse, 0.0)

        def reduce(high, low):
            row_high, row_low = row_of(high, step), row_of(low, step)
            taken = ratio * row_high
            error_taken = product_error(ratio_parts, split(row_high), taken)
            high, error = two_sum(high, -taken)
            low = low + error - error_taken - (ratio * row_low + ratio_low * row_high)
            return two_sum(high, low)

        own_high, own_low = reduce(next_high, next_low)
        high, low = reduce(high, low)

    diagonal = jnp.sum(jnp.where(wide == rows, high, 0.0), axis=1, keepdims=True)
    root = jnp.broadcast_to(jnp.sqrt(diagonal), shape)
    size = math.sqrt(count)
    upper = high / root
    factor[...] = jnp.where(wide >= rows, upper * (1.0 / size), 0.0)[:, :PROBES]
    inverse = upper * size
    columns = [
        jnp.broadcast_to(inverse[:, PROBES + index : PROBES + index + 1], shape) for index in range(PROBES)
    ]

    copies = []
    for level in range(LEVELS):
        for y in range(ROWS):
            outs = [None, None]
            for index in range(PROBES):
                value = image[y, level, index // 8, index % 8 : index % 8 + 1, :]
                for part in range(index // 8, 2):
                    term = columns[index][8 * part : 8 * part + 8] * value
                    outs[part] = term if outs[part] is None else outs[part] + term
            for part in range(2):
                held[level, pl.ds(part * 8 * ROWS + y, 8, stride=ROWS), :] = outs[part]
        copies.append(pltpu.make_async_copy(held.at[level], basis.at[level], sems.at[level]))
        copies[-1].start()
    for copy in copies:
        copy.wait()


def call(kernel, outs, scratch=(), inputs=pltpu.VMEM, spaces=None, cost=None):
    def run(*operands):
        return pl.pallas_call(
            kernel,
            out_shape=[jax.ShapeDtypeStruct(shape, F32) for shape in outs],
            in_specs=[pl.BlockSpec(memory_space=inputs)] * len(operands),
            out_specs=[pl.BlockSpec(memory_space=space) for space in spaces or [pltpu.VMEM] * len(outs)],
            scratch_shapes=list(scratch),
            cost_estimate=cost,
            compiler_params=pltpu.CompilerParams(vmem_limit_bytes=40 << 20),
        )(*operands)

    return run


def body(probes, winds, diffusivity, mixing, prior_scale, obs_weight):
    tile = (8, LANES)
    size_x, size_y = lax.axis_size("gx"), lax.axis_size("gy")
    count = LEVELS * ROWS * LANES * size_x * size_y

    def shift(value, axis, step):
        number = lax.axis_size(axis)
        pairs = [(i, i + step) for i in range(number) if 0 <= i + step < number]
        return lax.ppermute(value, axis, pairs)

    def exchange(message, axis):
        received = lax.all_to_all(message, axis, 0, 0)
        return received.reshape((message.shape[0] // 2,) + tile)

    flat = (LEVELS, PROBES * ROWS, LANES)
    source, east, west, fields, prior = call(
        pack_kernel,
        [(ROWS, LEVELS, 2) + tile, (X_PARTS,) + tile, (X_PARTS,) + tile, (FIELDS, ROWS, LANES), (LEVELS, ROWS, LANES)],
        [pltpu.VMEM(flat, F32), pltpu.SemaphoreType.DMA((7,))],
        pltpu.HBM,
    )(*(pltpu.with_memory_space_constraint(a, pltpu.HBM) for a in (probes.reshape(flat), winds, diffusivity, mixing, prior_scale, obs_weight)))
    from_west = shift(east, "gx", 1)
    from_east = shift(west, "gx", -1)
    halo, north, south = call(
        merge_kernel, [(X_PARTS,) + tile, (Y_PARTS,) + tile, (Y_PARTS,) + tile]
    )(from_west, from_east, source, fields)
    from_south = shift(north, "gy", 1)
    from_north = shift(south, "gy", -1)
    field = (ROWS, LEVELS, 3) + tile
    derived = (2, DERIVED, ROWS, LANES)
    values = HALO * math.prod(field)
    inner, coefs = call(
        inner_kernel,
        [(HALO,) + field, derived],
        cost=pl.CostEstimate(flops=20 * values, bytes_accessed=8 * values, transcendentals=0),
    )(source, halo, fields)
    image, message = call(
        stencil_kernel,
        [(ROWS, LEVELS, 2) + tile, (size_y, 4, LANES)],
        [
            pltpu.VMEM((HALO + 1,) + field, F32),
            pltpu.VMEM(derived, F32),
            pltpu.VMEM((ROWS, PROBES * SLICES, LEVELS * LANES), jnp.bfloat16),
        ],
    )(inner, coefs, prior, from_south, from_north)
    received = exchange(message, "gy")
    (message,) = call(sum_kernel, [(size_x, 4, LANES)])(received)
    received = exchange(message, "gx")
    basis, factor = call(
        lambda *refs: factor_kernel(count, *refs),
        [flat, (PROBES, PROBES)],
        [pltpu.VMEM(flat, F32), pltpu.SemaphoreType.DMA((LEVELS,))],
        spaces=[pltpu.HBM, pltpu.VMEM],
    )(received, image)
    return basis.reshape(probes.shape), factor


def solution(mesh):
    placed = (
        P(None, None, "gy", "gx"),
        P(None, None, "gy", "gx"),
        P(None, "gy", "gx"),
        P("gy", "gx"),
        P(None, "gy", "gx"),
        P(None, "gy", "gx"),
    )
    return jax.shard_map(
        body,
        mesh=mesh,
        in_specs=placed,
        out_specs=(P(None, None, "gy", "gx"), P()),
        check_vma=False,
    )
```

```python
import math
import jax
import jax.numpy as jnp
from jax import lax
from jax.experimental import pallas as pl
from jax.experimental.pallas import tpu as pltpu
from jax.sharding import PartitionSpec as P

STEPS = 4
LEVELS = 4
PROBES = 16
HALO = 2 * STEPS
LANES = 128
ROWS = 16
EXT = ROWS + 2 * HALO
F32 = jnp.float32

FIELDS = 17
GROUPS = 3
EAST, WEST, NORTH, SOUTH, CENTER, RATE, OBS, DERIVED = 0, 4, 8, 12, 16, 20, 21, 25
X_PARTS = ROWS + 2 * GROUPS
Y_SOURCE, Y_HALO, Y_COEF, Y_COEF_HALO, Y_PARTS = 0, 64, 72, 89, 92
SLICES = 4


def lane_ids():
    return lax.broadcasted_iota(jnp.int32, (8, LANES), 1)


def roll_lanes(value, shift):
    shift = shift % LANES
    return value if shift == 0 else pltpu.roll(value, shift, value.ndim - 1)


def pack_kernel(
    probes_in, winds_in, diffusivity_in, mixing_in, prior_in, obs_in,
    source, edges, fields, prior, probes, sems,
):
    coef_copies = [
        pltpu.make_async_copy(diffusivity_in, fields.at[pl.ds(0, 4)], sems.at[0]),
        pltpu.make_async_copy(winds_in.at[0], fields.at[pl.ds(4, 4)], sems.at[1]),
        pltpu.make_async_copy(winds_in.at[1], fields.at[pl.ds(8, 4)], sems.at[2]),
        pltpu.make_async_copy(obs_in, fields.at[pl.ds(12, 4)], sems.at[3]),
        pltpu.make_async_copy(mixing_in, fields.at[16], sems.at[4]),
    ]
    source_copies = [
        pltpu.make_async_copy(probes_in, probes, sems.at[5]),
        pltpu.make_async_copy(prior_in, prior, sems.at[6]),
    ]
    for copy in source_copies + coef_copies:
        copy.start()
    lanes = lane_ids()

    def put(held, value, slot):
        return jnp.where(lanes // 16 == slot, roll_lanes(value, 16 * slot + HALO), held)

    zero = jnp.zeros((8, LANES), F32)
    for copy in coef_copies:
        copy.wait()
    for group in range(GROUPS):
        for tile in range(2):
            held = zero
            for slot in range(8):
                field = 8 * group + slot
                if field < FIELDS:
                    held = put(held, fields[field, 8 * tile : 8 * tile + 8, :], slot)
            edges[ROWS + 2 * group + tile] = held
    for copy in source_copies:
        copy.wait()
    for y in range(ROWS):
        held = zero
        for level in range(LEVELS):
            scale = prior[level, y : y + 1, :]
            for part in range(2):
                value = probes[level, pl.ds(part * 8 * ROWS + y, 8, stride=ROWS), :] * scale
                source[y, level, part] = value
                held = put(held, value, 2 * level + part)
        edges[y] = held


def is_odd(axis):
    return lax.axis_index(axis) % 2


def merge_kernel(first, second, source, fields, halo, first_out, second_out):
    inner = lane_ids() % 16 < 8
    odd_x, odd_y = is_odd("gx"), is_odd("gy")
    for index in range(X_PARTS):
        from_east = jnp.where(odd_x == 0, first[index], second[index])
        from_west = jnp.where(odd_x == 0, second[index], first[index])
        halo[index] = jnp.where(inner, roll_lanes(from_east, -HALO), roll_lanes(from_west, HALO))
    for tile, out in ((1 - odd_y, first_out), (odd_y, second_out)):
        base = pl.multiple_of(8 * tile, 8)
        for y in range(8):
            for level in range(LEVELS):
                for part in range(2):
                    out[(y * LEVELS + level) * 2 + part] = source[base + y, level, part]
            out[Y_HALO + y] = halo[base + y]
        for field in range(FIELDS):
            out[Y_COEF + field] = fields[field, pl.ds(base, 8), :]
        for group in range(GROUPS):
            out[Y_COEF_HALO + group] = halo[ROWS + 2 * group + tile]


def strip_of(lanes, first, second, halo_first, halo_second, slot_first, slot_second):
    value = roll_lanes(first, 24)
    value = jnp.where(lanes >= 24, roll_lanes(halo_first, 24 - 16 * slot_first), value)
    value = jnp.where(lanes >= 40, roll_lanes(first, 40), value)
    value = jnp.where(lanes >= 64, roll_lanes(second, 88), value)
    value = jnp.where(lanes >= 88, roll_lanes(halo_second, 88 - 16 * slot_second), value)
    return jnp.where(lanes >= 104, roll_lanes(second, 104), value)


def two_sum(a, b):
    total = a + b
    other = total - a
    return total, (a - (total - other)) + (b - other)


def derive(coefs, rows, kind, values):
    rate = values[16]
    coefs[kind, RATE, rows, :] = rate
    for level in range(LEVELS):
        kappa, wind_x, wind_y = values[level], values[4 + level], values[8 + level]
        coefs[kind, EAST + level, rows, :] = kappa - wind_x
        coefs[kind, WEST + level, rows, :] = kappa + wind_x
        coefs[kind, NORTH + level, rows, :] = kappa - wind_y
        coefs[kind, SOUTH + level, rows, :] = kappa + wind_y
        sides = 1.0 if level in (0, LEVELS - 1) else 2.0
        coefs[kind, CENTER + level, rows, :] = 1.0 - 4.0 * kappa - sides * rate
        coefs[kind, OBS + level, rows, :] = values[12 + level]


def derive_both(coefs, tile, main, packed):
    lanes = lane_ids()
    strips = [
        strip_of(lanes, main[field], main[field], packed[field // 8], packed[field // 8], field % 8, field % 8)
        for field in range(FIELDS)
    ]
    for kind, values in ((0, main), (1, strips)):
        derive(coefs, slice(8 * tile, 8 * tile + 8), kind, values)


def vertical(values, level):
    if level == 0:
        return values[1]
    if level == LEVELS - 1:
        return values[LEVELS - 2]
    return values[level - 1] + values[level + 1]


def forward(get, coef_of, low, high, parts, emit):
    def load(y):
        return [[get(y, level, part) for level in range(LEVELS)] for part in parts]

    before, center = load(low - 1), load(low)
    for y in range(low, high):
        after = load(y + 1)
        coef = lambda index: coef_of(parts[0] // 2, index, y)
        rate = coef(RATE)
        results = [[None] * LEVELS for part in parts]
        for level in range(LEVELS):
            middle, east, west, north, south = [coef(base + level) for base in (CENTER, EAST, WEST, NORTH, SOUTH)]
            for index in range(len(parts)):
                value = center[index][level]
                results[index][level] = (
                    (middle * value + rate * vertical(center[index], level))
                    + (north * after[index][level] + south * before[index][level])
                    + (east * roll_lanes(value, -1) + west * roll_lanes(value, 1))
                )
        emit(y, parts, results)
        before, center = center, after


def adjoint(get, coef_of, low, high, parts, emit):
    def load(y):
        return [[get(y, level, part) for level in range(LEVELS)] for part in parts]

    def taken(base, y, values):
        own = [coef_of(parts[0] // 2, base + level, y) for level in range(LEVELS)]
        return [[own[level] * row[level] for level in range(LEVELS)] for row in values]

    pushed = taken(NORTH, low - 1, load(low - 1))
    partial = None
    for y in range(low, high + 1):
        center = load(y)
        if partial is not None:
            pulled = taken(SOUTH, y, center)
            emit(y - 1, parts, [
                [partial[index][level] + pulled[index][level] for level in range(LEVELS)] for index in range(len(parts))
            ])
        if y == high:
            break
        coef = lambda index: coef_of(parts[0] // 2, index, y)
        rate = coef(RATE)
        partial = [[None] * LEVELS for part in parts]
        for level in range(LEVELS):
            middle, east, west = [coef(base + level) for base in (CENTER, EAST, WEST)]
            for index in range(len(parts)):
                value = center[index][level]
                partial[index][level] = (
                    (middle * value + rate * vertical(center[index], level))
                    + (roll_lanes(west * value, -1) + roll_lanes(east * value, 1))
                    + pushed[index][level]
                )
        pushed = taken(NORTH, y, center)


GROUPED = ((2,), (0, 1))


def advance(step, low, high, get, put, coef_of):
    def emit(y, parts, results):
        for index, part in enumerate(parts):
            for level in range(LEVELS):
                value = results[index][level]
                if step < STEPS:
                    value = value + get(0, y, level, part)
                elif step == STEPS:
                    value = value * coef_of(part // 2, OBS + level, y)
                put(step, y, level, part, value)

    before = lambda y, level, part: get(step - 1, y, level, part)
    for parts in GROUPED:
        (forward if step <= STEPS else adjoint)(before, coef_of, low, high, parts, emit)


def inner_kernel(source, halo, fields, inner, coefs):
    lanes = lane_ids()
    for tile in range(2):
        main = [fields[field, 8 * tile : 8 * tile + 8, :] for field in range(FIELDS)]
        derive_both(coefs, tile, main, [halo[ROWS + 2 * group + tile] for group in range(GROUPS)])
    for y in range(ROWS):
        packed = halo[y]
        for level in range(LEVELS):
            low, high = source[y, level, 0], source[y, level, 1]
            inner[0, y, level, 0] = low
            inner[0, y, level, 1] = high
            inner[0, y, level, 2] = strip_of(lanes, low, high, packed, packed, 2 * level, 2 * level + 1)

    def get(step, y, level, part):
        return inner[step, y - HALO, level, part]

    def put(step, y, level, part, value):
        inner[step, y - HALO, level, part] = value

    def coef_of(kind, index, y):
        return coefs[kind, index, y - HALO : y - HALO + 1, :]

    for step in range(1, HALO):
        advance(step, HALO + step, HALO + ROWS - step, get, put, coef_of)


def stencil_kernel(inner, coefs, prior, first, second, image, message, outer, outer_coefs, slices):
    lanes = lane_ids()
    odd_y = is_odd("gy")
    for tile in range(2):
        def beside(index, tile=tile):
            return jnp.where(odd_y == tile, second[index], first[index])

        main = [beside(Y_COEF + field) for field in range(FIELDS)]
        derive_both(outer_coefs, tile, main, [beside(Y_COEF_HALO + group) for group in range(GROUPS)])
        for y in range(HALO):
            packed = beside(Y_HALO + y)
            for level in range(LEVELS):
                low, high = beside((y * LEVELS + level) * 2), beside((y * LEVELS + level) * 2 + 1)
                outer[0, HALO * tile + y, level, 0] = low
                outer[0, HALO * tile + y, level, 1] = high
                outer[0, HALO * tile + y, level, 2] = strip_of(lanes, low, high, packed, packed, 2 * level, 2 * level + 1)

    def place(step, y):
        if y < HALO + step:
            return outer, y - step
        if y >= HALO + ROWS - step:
            return outer, HALO + y - (HALO + ROWS - step)
        return inner, y - HALO

    def get(step, y, level, part):
        ref, row = place(step, y)
        return ref[step, row, level, part]

    def put(step, y, level, part, value):
        ref, row = place(step, y)
        ref[step, row, level, part] = value

    def coef_of(kind, index, y):
        if y < HALO:
            return outer_coefs[kind, index, y : y + 1, :]
        if y >= HALO + ROWS:
            return outer_coefs[kind, index, y - ROWS : y - ROWS + 1, :]
        return coefs[kind, index, y - HALO : y - HALO + 1, :]

    for step in range(1, HALO):
        advance(step, step, step + HALO, get, put, coef_of)
        advance(step, EXT - HALO - step, EXT - step, get, put, coef_of)

    zero = jnp.zeros((8, LANES), F32)
    most = [zero, zero]

    def total_of(y, part, level, value):
        first, second, third = [get(step, y, level, part) for step in range(STEPS + 1, 2 * STEPS)]
        return (first + second) + (third + value)

    def emit_last(y, parts, results):
        for level in range(LEVELS):
            if parts == (2,):
                outer[2 * STEPS, y - HALO, level, 2] = total_of(y, 2, level, results[0][level])
                continue
            scale = prior[level, y - HALO : y - HALO + 1, :]
            strip = outer[2 * STEPS, y - HALO, level, 2]
            for part in parts:
                value = total_of(y, part, level, results[part][level])
                value = jnp.where(lanes < HALO, roll_lanes(strip, -40 - 64 * part), value)
                value = jnp.where(lanes >= LANES - HALO, roll_lanes(strip, 104 - 64 * part), value)
                value = value * scale
                image[y - HALO, level, part] = value
                most[part] = jnp.maximum(most[part], jnp.abs(value))

    for parts in GROUPED:
        adjoint(lambda y, level, part: get(2 * STEPS - 1, y, level, part), coef_of, HALO, HALO + ROWS, parts, emit_last)

    magics = []
    for part in range(2):
        top = jnp.broadcast_to(jnp.max(most[part], axis=1, keepdims=True), (8, LANES))
        scaled = top * (2.0**23 + 1.0)
        power = jnp.abs(scaled - scaled * (1.0 - 2.0**-24))
        magics.append([power * (1.5 * 2.0 ** (23 - 6 - 8 * index)) for index in range(SLICES)])

    def slice_row(y, carry):
        for level in range(LEVELS):
            pieces = []
            for part in range(2):
                rest = image[y, level, part]
                own = []
                for index in range(SLICES):
                    magic = magics[part][index]
                    piece = (rest + magic) - magic
                    rest = rest - piece
                    own.append(piece)
                pieces.append(own)
            for index in range(SLICES):
                both = jnp.concatenate([pieces[0][index], pieces[1][index]], axis=0)
                slices[y, pl.ds(PROBES * index, PROBES), pl.ds(LANES * level, LANES)] = both.astype(jnp.bfloat16)
        return carry

    lax.fori_loop(0, ROWS, slice_row, 0, unroll=True)

    width = PROBES * SLICES
    high = jnp.zeros((width, width), F32)
    low = jnp.zeros((width, width), F32)
    for pair in range(ROWS // 2):
        block = jnp.concatenate([slices[2 * pair], slices[2 * pair + 1]], axis=1)
        product = lax.dot_general(block, block, (((1,), (1,)), ((), ())), preferred_element_type=F32)
        high, error = two_sum(high, product)
        low = low + error

    def fold(high, low, blocks):
        total_high, total_low = None, None
        for block_high, block_low in blocks(high, low):
            if total_high is None:
                total_high, total_low = block_high, block_low
            else:
                total_high, error = two_sum(total_high, block_high)
                total_low = total_low + block_low + error
        return total_high, total_low

    def row_blocks(high, low):
        for index in range(SLICES):
            rows = slice(PROBES * index, PROBES * (index + 1))
            yield high[rows], low[rows]

    def lane_blocks(high, low):
        for index in range(SLICES):
            yield roll_lanes(high, -PROBES * index), roll_lanes(low, -PROBES * index)

    high, low = fold(high, low, row_blocks)
    rest = jnp.zeros((PROBES, LANES - width), F32)
    high, low = jnp.concatenate([high, rest], axis=1), jnp.concatenate([low, rest], axis=1)
    high, low = fold(high, low, lane_blocks)
    high, low = two_sum(high, low)

    wide = lax.broadcasted_iota(jnp.int32, (PROBES, LANES), 1)
    both = jnp.where(wide < PROBES, high, roll_lanes(low, PROBES))
    packed = both[0:8]
    for index in range(1, 4):
        value = both[8 * (index // 2) : 8 * (index // 2) + 8]
        if index % 2:
            value = pltpu.roll(value, 4, 0)
        packed = jnp.where(lanes // 32 == index, roll_lanes(value, 32 * index), packed)
    message[...] = jnp.broadcast_to(packed[None, 0:4], message.shape)


def split(a):
    scaled = a * 4097.0
    high = scaled - (scaled - a)
    return high, a - high


def product_error(a, b, product):
    a_high, a_low = a
    b_high, b_low = b
    return ((a_high * b_high - product) + a_high * b_low + a_low * b_high) + a_low * b_low


def summed(received):
    zero = jnp.zeros((8, LANES), F32)
    chains = 4
    sums, errors = [zero] * chains, [zero] * chains
    for index in range(received.shape[0]):
        chain = index % chains
        sums[chain], error = two_sum(sums[chain], received[index])
        errors[chain] = errors[chain] + error
    total, rest = sums[0], errors[0]
    for chain in range(1, chains):
        total, error = two_sum(total, sums[chain])
        rest = rest + errors[chain] + error
    total, error = two_sum(total, pltpu.roll(total, 4, 0))
    return total, rest + pltpu.roll(rest, 4, 0) + error


def sum_kernel(received, message):
    total, rest = summed(received)
    total = total + jnp.where(lane_ids() % 32 < PROBES, 0.0, roll_lanes(rest, PROBES))
    message[...] = jnp.broadcast_to(total[None, 0:4], message.shape)


def factor_kernel(count, received, image, basis, factor, held, sems):
    upper_half = lax.broadcasted_iota(jnp.int32, (8, LANES), 0) < 4
    total, rest = summed(received)
    rest = rest + roll_lanes(total, -PROBES)

    def unpack(value):
        low = jnp.where(upper_half, value, roll_lanes(value, -32))
        high = jnp.where(upper_half, roll_lanes(value, -64), roll_lanes(value, -96))
        return jnp.concatenate([low, high], axis=0)

    high, low = two_sum(unpack(total), unpack(rest))

    shape = (PROBES, LANES)
    wide = lax.broadcasted_iota(jnp.int32, shape, 1)
    rows = lax.broadcasted_iota(jnp.int32, shape, 0)
    high = jnp.where(wide < PROBES, high, jnp.where(wide == rows + PROBES, 1.0, 0.0))
    low = jnp.where(wide < PROBES, low, 0.0)

    def column(index):
        return [jnp.broadcast_to(value[:, index : index + 1], shape) for value in (high, low)]

    def row_of(value, index):
        return jnp.broadcast_to(value[index : index + 1], shape)

    own_high, own_low = column(0)
    for step in range(PROBES - 1):
        next_high, next_low = column(step + 1)
        pivot_high, pivot_low = row_of(own_high, step), row_of(own_low, step)
        inverse = 1.0 / pivot_high
        ratio = jnp.where(rows > step, own_high * inverse, 0.0)
        ratio_parts = split(ratio)
        taken = ratio * pivot_high
        remainder = ((own_high - taken) - product_error(ratio_parts, split(pivot_high), taken)) + (
            own_low - ratio * pivot_low
        )
        ratio_low = jnp.where(rows > step, remainder * inverse, 0.0)

        def reduce(high, low):
            row_high, row_low = row_of(high, step), row_of(low, step)
            taken = ratio * row_high
            error_taken = product_error(ratio_parts, split(row_high), taken)
            high, error = two_sum(high, -taken)
            low = low + error - error_taken - (ratio * row_low + ratio_low * row_high)
            return two_sum(high, low)

        own_high, own_low = reduce(next_high, next_low)
        high, low = reduce(high, low)

    diagonal = jnp.sum(jnp.where(wide == rows, high, 0.0), axis=1, keepdims=True)
    root = jnp.broadcast_to(jnp.sqrt(diagonal), shape)
    size = math.sqrt(count)
    upper = high / root
    factor[...] = jnp.where(wide >= rows, upper * (1.0 / size), 0.0)[:, :PROBES]
    inverse = upper * size
    columns = [
        jnp.broadcast_to(inverse[:, PROBES + index : PROBES + index + 1], shape) for index in range(PROBES)
    ]

    copies = []
    for level in range(LEVELS):
        for y in range(ROWS):
            outs = [None, None]
            for index in range(PROBES):
                value = image[y, level, index // 8, index % 8 : index % 8 + 1, :]
                for part in range(index // 8, 2):
                    term = columns[index][8 * part : 8 * part + 8] * value
                    outs[part] = term if outs[part] is None else outs[part] + term
            for part in range(2):
                held[level, pl.ds(part * 8 * ROWS + y, 8, stride=ROWS), :] = outs[part]
        copies.append(pltpu.make_async_copy(held.at[level], basis.at[level], sems.at[level]))
        copies[-1].start()
    for copy in copies:
        copy.wait()


def call(kernel, outs, scratch=(), inputs=pltpu.VMEM, spaces=None, cost=None):
    def run(*operands):
        return pl.pallas_call(
            kernel,
            out_shape=[jax.ShapeDtypeStruct(shape, F32) for shape in outs],
            in_specs=[pl.BlockSpec(memory_space=inputs)] * len(operands),
            out_specs=[pl.BlockSpec(memory_space=space) for space in spaces or [pltpu.VMEM] * len(outs)],
            scratch_shapes=list(scratch),
            cost_estimate=cost,
            compiler_params=pltpu.CompilerParams(vmem_limit_bytes=40 << 20),
        )(*operands)

    return run


def body(probes, winds, diffusivity, mixing, prior_scale, obs_weight):
    tile = (8, LANES)
    size_x, size_y = lax.axis_size("gx"), lax.axis_size("gy")
    count = LEVELS * ROWS * LANES * size_x * size_y

    def swap(value, axis, start):
        pairs = [(i, i + 1) for i in range(start, lax.axis_size(axis) - 1, 2)]
        return lax.ppermute(value, axis, pairs + [(j, i) for i, j in pairs])

    def exchange(message, axis):
        received = lax.all_to_all(message, axis, 0, 0)
        return received.reshape((message.shape[0] // 2,) + tile)

    flat = (LEVELS, PROBES * ROWS, LANES)
    source, edges, fields, prior = call(
        pack_kernel,
        [(ROWS, LEVELS, 2) + tile, (X_PARTS,) + tile, (FIELDS, ROWS, LANES), (LEVELS, ROWS, LANES)],
        [pltpu.VMEM(flat, F32), pltpu.SemaphoreType.DMA((7,))],
        pltpu.HBM,
    )(*(pltpu.with_memory_space_constraint(a, pltpu.HBM) for a in (probes.reshape(flat), winds, diffusivity, mixing, prior_scale, obs_weight)))
    halo, first, second = call(
        merge_kernel, [(X_PARTS,) + tile, (Y_PARTS,) + tile, (Y_PARTS,) + tile]
    )(swap(edges, "gx", 0), swap(edges, "gx", 1), source, fields)
    first, second = swap(first, "gy", 0), swap(second, "gy", 1)
    field = (ROWS, LEVELS, 3) + tile
    derived = (2, DERIVED, ROWS, LANES)
    values = HALO * math.prod(field)
    inner, coefs = call(
        inner_kernel,
        [(HALO,) + field, derived],
        cost=pl.CostEstimate(flops=20 * values, bytes_accessed=8 * values, transcendentals=0),
    )(source, halo, fields)
    image, message = call(
        stencil_kernel,
        [(ROWS, LEVELS, 2) + tile, (size_y, 4, LANES)],
        [
            pltpu.VMEM((HALO + 1,) + field, F32),
            pltpu.VMEM(derived, F32),
            pltpu.VMEM((ROWS, PROBES * SLICES, LEVELS * LANES), jnp.bfloat16),
        ],
    )(inner, coefs, prior, first, second)
    received = exchange(message, "gy")
    (message,) = call(sum_kernel, [(size_x, 4, LANES)])(received)
    received = exchange(message, "gx")
    basis, factor = call(
        lambda *refs: factor_kernel(count, *refs),
        [flat, (PROBES, PROBES)],
        [pltpu.VMEM(flat, F32), pltpu.SemaphoreType.DMA((LEVELS,))],
        spaces=[pltpu.HBM, pltpu.VMEM],
    )(received, image)
    return basis.reshape(probes.shape), factor


def solution(mesh):
    placed = (
        P(None, None, "gy", "gx"),
        P(None, None, "gy", "gx"),
        P(None, "gy", "gx"),
        P("gy", "gx"),
        P(None, "gy", "gx"),
        P(None, "gy", "gx"),
    )
    return jax.shard_map(
        body,
        mesh=mesh,
        in_specs=placed,
        out_specs=(P(None, None, "gy", "gx"), P()),
        check_vma=False,
    )
```

```python
import math
import jax
import jax.numpy as jnp
from jax import lax
from jax.experimental import pallas as pl
from jax.experimental.pallas import tpu as pltpu
from jax.sharding import PartitionSpec as P

STEPS = 4
LEVELS = 4
PROBES = 16
HALO = 2 * STEPS
LANES = 128
ROWS = 16
EXT = ROWS + 2 * HALO
F32 = jnp.float32

FIELDS = 17
GROUPS = 3
EAST, WEST, NORTH, SOUTH, CENTER, RATE, OBS, DERIVED = 0, 4, 8, 12, 16, 20, 21, 25
X_PARTS = ROWS + 2 * GROUPS
Y_SOURCE, Y_HALO, Y_COEF, Y_COEF_HALO, Y_PARTS = 0, 64, 72, 89, 92
SLICES = 4


def lane_ids():
    return lax.broadcasted_iota(jnp.int32, (8, LANES), 1)


def roll_lanes(value, shift):
    shift = shift % LANES
    return value if shift == 0 else pltpu.roll(value, shift, value.ndim - 1)


def pack_kernel(
    probes_in, winds_in, diffusivity_in, mixing_in, prior_in, obs_in,
    source, edges, fields, prior, probes, sems,
):
    coef_copies = [
        pltpu.make_async_copy(diffusivity_in, fields.at[pl.ds(0, 4)], sems.at[0]),
        pltpu.make_async_copy(winds_in.at[0], fields.at[pl.ds(4, 4)], sems.at[1]),
        pltpu.make_async_copy(winds_in.at[1], fields.at[pl.ds(8, 4)], sems.at[2]),
        pltpu.make_async_copy(obs_in, fields.at[pl.ds(12, 4)], sems.at[3]),
        pltpu.make_async_copy(mixing_in, fields.at[16], sems.at[4]),
    ]
    source_copies = [
        pltpu.make_async_copy(probes_in, probes, sems.at[5]),
        pltpu.make_async_copy(prior_in, prior, sems.at[6]),
    ]
    for copy in source_copies + coef_copies:
        copy.start()
    lanes = lane_ids()

    def put(held, value, slot):
        return jnp.where(lanes // 16 == slot, roll_lanes(value, 16 * slot + HALO), held)

    zero = jnp.zeros((8, LANES), F32)
    for copy in coef_copies:
        copy.wait()
    for group in range(GROUPS):
        for tile in range(2):
            held = zero
            for slot in range(8):
                field = 8 * group + slot
                if field < FIELDS:
                    held = put(held, fields[field, 8 * tile : 8 * tile + 8, :], slot)
            edges[ROWS + 2 * group + tile] = held
    for copy in source_copies:
        copy.wait()
    for y in range(ROWS):
        held = zero
        for level in range(LEVELS):
            scale = prior[level, y : y + 1, :]
            for part in range(2):
                value = probes[level, pl.ds(part * 8 * ROWS + y, 8, stride=ROWS), :] * scale
                source[y, level, part] = value
                held = put(held, value, 2 * level + part)
        edges[y] = held


def is_odd(axis):
    return lax.axis_index(axis) % 2


def merge_kernel(first, second, source, fields, halo, first_out, second_out):
    inner = lane_ids() % 16 < 8
    odd_x, odd_y = is_odd("gx"), is_odd("gy")
    for index in range(X_PARTS):
        from_east = jnp.where(odd_x == 0, first[index], second[index])
        from_west = jnp.where(odd_x == 0, second[index], first[index])
        halo[index] = jnp.where(inner, roll_lanes(from_east, -HALO), roll_lanes(from_west, HALO))
    for tile, out in ((1 - odd_y, first_out), (odd_y, second_out)):
        base = pl.multiple_of(8 * tile, 8)
        for y in range(8):
            for level in range(LEVELS):
                for part in range(2):
                    out[(y * LEVELS + level) * 2 + part] = source[base + y, level, part]
            out[Y_HALO + y] = halo[base + y]
        for field in range(FIELDS):
            out[Y_COEF + field] = fields[field, pl.ds(base, 8), :]
        for group in range(GROUPS):
            out[Y_COEF_HALO + group] = halo[ROWS + 2 * group + tile]


def strip_of(lanes, first, second, halo_first, halo_second, slot_first, slot_second):
    value = roll_lanes(first, 24)
    value = jnp.where(lanes >= 24, roll_lanes(halo_first, 24 - 16 * slot_first), value)
    value = jnp.where(lanes >= 40, roll_lanes(first, 40), value)
    value = jnp.where(lanes >= 64, roll_lanes(second, 88), value)
    value = jnp.where(lanes >= 88, roll_lanes(halo_second, 88 - 16 * slot_second), value)
    return jnp.where(lanes >= 104, roll_lanes(second, 104), value)


def two_sum(a, b):
    total = a + b
    other = total - a
    return total, (a - (total - other)) + (b - other)


def derive(coefs, rows, kind, values):
    rate = values[16]
    coefs[kind, RATE, rows, :] = rate
    for level in range(LEVELS):
        kappa, wind_x, wind_y = values[level], values[4 + level], values[8 + level]
        coefs[kind, EAST + level, rows, :] = kappa - wind_x
        coefs[kind, WEST + level, rows, :] = kappa + wind_x
        coefs[kind, NORTH + level, rows, :] = kappa - wind_y
        coefs[kind, SOUTH + level, rows, :] = kappa + wind_y
        sides = 1.0 if level in (0, LEVELS - 1) else 2.0
        coefs[kind, CENTER + level, rows, :] = 1.0 - 4.0 * kappa - sides * rate
        coefs[kind, OBS + level, rows, :] = values[12 + level]


def derive_both(coefs, tile, main, packed):
    lanes = lane_ids()
    strips = [
        strip_of(lanes, main[field], main[field], packed[field // 8], packed[field // 8], field % 8, field % 8)
        for field in range(FIELDS)
    ]
    for kind, values in ((0, main), (1, strips)):
        derive(coefs, slice(8 * tile, 8 * tile + 8), kind, values)


def vertical(values, level):
    if level == 0:
        return values[1]
    if level == LEVELS - 1:
        return values[LEVELS - 2]
    return values[level - 1] + values[level + 1]


def forward(get, coef_of, low, high, parts, emit):
    def load(y):
        return [[get(y, level, part) for level in range(LEVELS)] for part in parts]

    before, center = load(low - 1), load(low)
    for y in range(low, high):
        after = load(y + 1)
        coef = lambda index: coef_of(parts[0] // 2, index, y)
        rate = coef(RATE)
        results = [[None] * LEVELS for part in parts]
        for level in range(LEVELS):
            middle, east, west, north, south = [coef(base + level) for base in (CENTER, EAST, WEST, NORTH, SOUTH)]
            for index in range(len(parts)):
                value = center[index][level]
                results[index][level] = (
                    (middle * value + rate * vertical(center[index], level))
                    + (north * after[index][level] + south * before[index][level])
                    + (east * roll_lanes(value, -1) + west * roll_lanes(value, 1))
                )
        emit(y, parts, results)
        before, center = center, after


def adjoint(get, coef_of, low, high, parts, emit):
    def load(y):
        return [[get(y, level, part) for level in range(LEVELS)] for part in parts]

    def taken(base, y, values):
        own = [coef_of(parts[0] // 2, base + level, y) for level in range(LEVELS)]
        return [[own[level] * row[level] for level in range(LEVELS)] for row in values]

    pushed = taken(NORTH, low - 1, load(low - 1))
    partial = None
    for y in range(low, high + 1):
        center = load(y)
        if partial is not None:
            pulled = taken(SOUTH, y, center)
            emit(y - 1, parts, [
                [partial[index][level] + pulled[index][level] for level in range(LEVELS)] for index in range(len(parts))
            ])
        if y == high:
            break
        coef = lambda index: coef_of(parts[0] // 2, index, y)
        rate = coef(RATE)
        partial = [[None] * LEVELS for part in parts]
        for level in range(LEVELS):
            middle, east, west = [coef(base + level) for base in (CENTER, EAST, WEST)]
            for index in range(len(parts)):
                value = center[index][level]
                partial[index][level] = (
                    (middle * value + rate * vertical(center[index], level))
                    + (roll_lanes(west * value, -1) + roll_lanes(east * value, 1))
                    + pushed[index][level]
                )
        pushed = taken(NORTH, y, center)


GROUPED = ((2,), (0, 1))


def advance(step, low, high, get, put, coef_of):
    def emit(y, parts, results):
        for index, part in enumerate(parts):
            for level in range(LEVELS):
                value = results[index][level]
                if step < STEPS:
                    value = value + get(0, y, level, part)
                elif step == STEPS:
                    value = value * coef_of(part // 2, OBS + level, y)
                put(step, y, level, part, value)

    before = lambda y, level, part: get(step - 1, y, level, part)
    for parts in GROUPED:
        (forward if step <= STEPS else adjoint)(before, coef_of, low, high, parts, emit)


def inner_kernel(source, halo, fields, inner, coefs):
    lanes = lane_ids()
    for tile in range(2):
        main = [fields[field, 8 * tile : 8 * tile + 8, :] for field in range(FIELDS)]
        derive_both(coefs, tile, main, [halo[ROWS + 2 * group + tile] for group in range(GROUPS)])
    for y in range(ROWS):
        packed = halo[y]
        for level in range(LEVELS):
            low, high = source[y, level, 0], source[y, level, 1]
            inner[0, y, level, 0] = low
            inner[0, y, level, 1] = high
            inner[0, y, level, 2] = strip_of(lanes, low, high, packed, packed, 2 * level, 2 * level + 1)

    def get(step, y, level, part):
        return inner[step, y - HALO, level, part]

    def put(step, y, level, part, value):
        inner[step, y - HALO, level, part] = value

    def coef_of(kind, index, y):
        return coefs[kind, index, y - HALO : y - HALO + 1, :]

    for step in range(1, HALO):
        advance(step, HALO + step, HALO + ROWS - step, get, put, coef_of)


def side(tile, received, inner, coefs, prior, image, most_out, outer, outer_coefs):
    lanes = lane_ids()
    main = [received[Y_COEF + field] for field in range(FIELDS)]
    derive_both(outer_coefs, 0, main, [received[Y_COEF_HALO + group] for group in range(GROUPS)])
    for y in range(HALO):
        packed = received[Y_HALO + y]
        for level in range(LEVELS):
            low, high = received[(y * LEVELS + level) * 2], received[(y * LEVELS + level) * 2 + 1]
            outer[0, y, level, 0] = low
            outer[0, y, level, 1] = high
            outer[0, y, level, 2] = strip_of(lanes, low, high, packed, packed, 2 * level, 2 * level + 1)

    def first_row(step):
        return EXT - HALO - step if tile else step

    def place(step, y):
        base = first_row(step)
        return (outer, y - base) if base <= y < base + HALO else (inner, y - HALO)

    def get(step, y, level, part):
        ref, row = place(step, y)
        return ref[step, row, level, part]

    def put(step, y, level, part, value):
        ref, row = place(step, y)
        ref[step, row, level, part] = value

    def coef_of(kind, index, y):
        base = first_row(0)
        if base <= y < base + HALO:
            return outer_coefs[kind, index, y - base : y - base + 1, :]
        return coefs[kind, index, y - HALO : y - HALO + 1, :]

    for step in range(1, HALO):
        advance(step, first_row(step), first_row(step) + HALO, get, put, coef_of)

    most = [jnp.zeros((8, LANES), F32)] * 2
    last = first_row(HALO)

    def total_of(y, part, level, value):
        first, second, third = [get(step, y, level, part) for step in range(STEPS + 1, 2 * STEPS)]
        return (first + second) + (third + value)

    def emit_last(y, parts, results):
        for level in range(LEVELS):
            if parts == (2,):
                outer[HALO, y - last, level, 2] = total_of(y, 2, level, results[0][level])
                continue
            scale = prior[level, y - HALO : y - HALO + 1, :]
            strip = outer[HALO, y - last, level, 2]
            for part in parts:
                value = total_of(y, part, level, results[part][level])
                value = jnp.where(lanes < HALO, roll_lanes(strip, -40 - 64 * part), value)
                value = jnp.where(lanes >= LANES - HALO, roll_lanes(strip, 104 - 64 * part), value)
                value = value * scale
                image[y - last, level, part] = value
                most[part] = jnp.maximum(most[part], jnp.abs(value))

    for parts in GROUPED:
        adjoint(lambda y, level, part: get(HALO - 1, y, level, part), coef_of, last, last + HALO, parts, emit_last)
    for part in range(2):
        most_out[part] = most[part]


def both_sides(first, args):
    odd_y = is_odd("gy")
    for tile in range(2):
        @pl.when(odd_y == (1 - tile if first else tile))
        def _(tile=tile):
            side(tile, *args)


def gram_pieces(image, most, slices, high, low):
    magics = []
    for part in range(2):
        top = jnp.broadcast_to(jnp.max(most[part], axis=1, keepdims=True), (8, LANES))
        scaled = top * (2.0**23 + 1.0)
        power = jnp.abs(scaled - scaled * (1.0 - 2.0**-24))
        magics.append([power * (1.5 * 2.0 ** (23 - 6 - 8 * index)) for index in range(SLICES)])
    for y in range(HALO):
        for level in range(LEVELS):
            pieces = []
            for part in range(2):
                rest = image[y, level, part]
                own = []
                for index in range(SLICES):
                    magic = magics[part][index]
                    piece = (rest + magic) - magic
                    rest = rest - piece
                    own.append(piece)
                pieces.append(own)
            for index in range(SLICES):
                both = jnp.concatenate([pieces[0][index], pieces[1][index]], axis=0)
                slices[y, pl.ds(PROBES * index, PROBES), pl.ds(LANES * level, LANES)] = both.astype(jnp.bfloat16)
    for pair in range(HALO // 2):
        block = jnp.concatenate([slices[2 * pair], slices[2 * pair + 1]], axis=1)
        product = lax.dot_general(block, block, (((1,), (1,)), ((), ())), preferred_element_type=F32)
        high, error = two_sum(high, product)
        low = low + error
    return high, low


def near_kernel(inner, coefs, prior, received, image, high_out, low_out, outer, outer_coefs, slices, most):
    both_sides(True, (received, inner, coefs, prior, image, most, outer, outer_coefs))
    zero = jnp.zeros(high_out.shape, F32)
    high_out[...], low_out[...] = gram_pieces(image, most, slices, zero, zero)


def far_kernel(
    inner, coefs, prior, received, high_in, low_in, image, message, outer, outer_coefs, slices, most
):
    lanes = lane_ids()
    both_sides(False, (received, inner, coefs, prior, image, most, outer, outer_coefs))
    high, low = gram_pieces(image, most, slices, high_in[...], low_in[...])
    width = PROBES * SLICES

    def fold(high, low, blocks):
        total_high, total_low = None, None
        for block_high, block_low in blocks(high, low):
            if total_high is None:
                total_high, total_low = block_high, block_low
            else:
                total_high, error = two_sum(total_high, block_high)
                total_low = total_low + block_low + error
        return total_high, total_low

    def row_blocks(high, low):
        for index in range(SLICES):
            rows = slice(PROBES * index, PROBES * (index + 1))
            yield high[rows], low[rows]

    def lane_blocks(high, low):
        for index in range(SLICES):
            yield roll_lanes(high, -PROBES * index), roll_lanes(low, -PROBES * index)

    high, low = fold(high, low, row_blocks)
    rest = jnp.zeros((PROBES, LANES - width), F32)
    high, low = jnp.concatenate([high, rest], axis=1), jnp.concatenate([low, rest], axis=1)
    high, low = fold(high, low, lane_blocks)
    high, low = two_sum(high, low)

    wide = lax.broadcasted_iota(jnp.int32, (PROBES, LANES), 1)
    both = jnp.where(wide < PROBES, high, roll_lanes(low, PROBES))
    packed = both[0:8]
    for index in range(1, 4):
        value = both[8 * (index // 2) : 8 * (index // 2) + 8]
        if index % 2:
            value = pltpu.roll(value, 4, 0)
        packed = jnp.where(lanes // 32 == index, roll_lanes(value, 32 * index), packed)
    message[...] = jnp.broadcast_to(packed[None, 0:4], message.shape)


def split(a):
    scaled = a * 4097.0
    high = scaled - (scaled - a)
    return high, a - high


def product_error(a, b, product):
    a_high, a_low = a
    b_high, b_low = b
    return ((a_high * b_high - product) + a_high * b_low + a_low * b_high) + a_low * b_low


def summed(received):
    zero = jnp.zeros((8, LANES), F32)
    chains = 4
    sums, errors = [zero] * chains, [zero] * chains
    for index in range(received.shape[0]):
        chain = index % chains
        sums[chain], error = two_sum(sums[chain], received[index])
        errors[chain] = errors[chain] + error
    total, rest = sums[0], errors[0]
    for chain in range(1, chains):
        total, error = two_sum(total, sums[chain])
        rest = rest + errors[chain] + error
    total, error = two_sum(total, pltpu.roll(total, 4, 0))
    return total, rest + pltpu.roll(rest, 4, 0) + error


def sum_kernel(received, message):
    total, rest = summed(received)
    total = total + jnp.where(lane_ids() % 32 < PROBES, 0.0, roll_lanes(rest, PROBES))
    message[...] = jnp.broadcast_to(total[None, 0:4], message.shape)


def factor_kernel(count, received, near, far, basis, factor, held, sems):
    upper_half = lax.broadcasted_iota(jnp.int32, (8, LANES), 0) < 4
    total, rest = summed(received)
    rest = rest + roll_lanes(total, -PROBES)

    def unpack(value):
        low = jnp.where(upper_half, value, roll_lanes(value, -32))
        high = jnp.where(upper_half, roll_lanes(value, -64), roll_lanes(value, -96))
        return jnp.concatenate([low, high], axis=0)

    high, low = two_sum(unpack(total), unpack(rest))

    shape = (PROBES, LANES)
    wide = lax.broadcasted_iota(jnp.int32, shape, 1)
    rows = lax.broadcasted_iota(jnp.int32, shape, 0)
    high = jnp.where(wide < PROBES, high, jnp.where(wide == rows + PROBES, 1.0, 0.0))
    low = jnp.where(wide < PROBES, low, 0.0)

    def column(index):
        return [jnp.broadcast_to(value[:, index : index + 1], shape) for value in (high, low)]

    def row_of(value, index):
        return jnp.broadcast_to(value[index : index + 1], shape)

    own_high, own_low = column(0)
    for step in range(PROBES - 1):
        next_high, next_low = column(step + 1)
        pivot_high, pivot_low = row_of(own_high, step), row_of(own_low, step)
        inverse = 1.0 / pivot_high
        ratio = jnp.where(rows > step, own_high * inverse, 0.0)
        ratio_parts = split(ratio)
        taken = ratio * pivot_high
        remainder = ((own_high - taken) - product_error(ratio_parts, split(pivot_high), taken)) + (
            own_low - ratio * pivot_low
        )
        ratio_low = jnp.where(rows > step, remainder * inverse, 0.0)

        def reduce(high, low):
            row_high, row_low = row_of(high, step), row_of(low, step)
            taken = ratio * row_high
            error_taken = product_error(ratio_parts, split(row_high), taken)
            high, error = two_sum(high, -taken)
            low = low + error - error_taken - (ratio * row_low + ratio_low * row_high)
            return two_sum(high, low)

        own_high, own_low = reduce(next_high, next_low)
        high, low = reduce(high, low)

    diagonal = jnp.sum(jnp.where(wide == rows, high, 0.0), axis=1, keepdims=True)
    root = jnp.broadcast_to(jnp.sqrt(diagonal), shape)
    size = math.sqrt(count)
    upper = high / root
    factor[...] = jnp.where(wide >= rows, upper * (1.0 / size), 0.0)[:, :PROBES]
    inverse = upper * size
    columns = [
        jnp.broadcast_to(inverse[:, PROBES + index : PROBES + index + 1], shape) for index in range(PROBES)
    ]

    copies = []
    odd_y = is_odd("gy")
    for level in range(LEVELS):
        for image, base in ((near, 8 * (1 - odd_y)), (far, 8 * odd_y)):
            for y in range(HALO):
                outs = [None, None]
                for index in range(PROBES):
                    value = image[y, level, index // 8, index % 8 : index % 8 + 1, :]
                    for part in range(index // 8, 2):
                        term = columns[index][8 * part : 8 * part + 8] * value
                        outs[part] = term if outs[part] is None else outs[part] + term
                for part in range(2):
                    held[level, pl.ds(base + (part * 8 * ROWS + y), 8, stride=ROWS), :] = outs[part]
        copies.append(pltpu.make_async_copy(held.at[level], basis.at[level], sems.at[level]))
        copies[-1].start()
    for copy in copies:
        copy.wait()


def call(kernel, outs, scratch=(), inputs=pltpu.VMEM, spaces=None, cost=None):
    def run(*operands):
        return pl.pallas_call(
            kernel,
            out_shape=[jax.ShapeDtypeStruct(shape, F32) for shape in outs],
            in_specs=[pl.BlockSpec(memory_space=inputs)] * len(operands),
            out_specs=[pl.BlockSpec(memory_space=space) for space in spaces or [pltpu.VMEM] * len(outs)],
            scratch_shapes=list(scratch),
            cost_estimate=cost,
            compiler_params=pltpu.CompilerParams(vmem_limit_bytes=40 << 20),
        )(*operands)

    return run


def body(probes, winds, diffusivity, mixing, prior_scale, obs_weight):
    tile = (8, LANES)
    size_x, size_y = lax.axis_size("gx"), lax.axis_size("gy")
    count = LEVELS * ROWS * LANES * size_x * size_y

    def swap(value, axis, start):
        pairs = [(i, i + 1) for i in range(start, lax.axis_size(axis) - 1, 2)]
        return lax.ppermute(value, axis, pairs + [(j, i) for i, j in pairs])

    def exchange(message, axis):
        received = lax.all_to_all(message, axis, 0, 0)
        return received.reshape((message.shape[0] // 2,) + tile)

    flat = (LEVELS, PROBES * ROWS, LANES)
    source, edges, fields, prior = call(
        pack_kernel,
        [(ROWS, LEVELS, 2) + tile, (X_PARTS,) + tile, (FIELDS, ROWS, LANES), (LEVELS, ROWS, LANES)],
        [pltpu.VMEM(flat, F32), pltpu.SemaphoreType.DMA((7,))],
        pltpu.HBM,
    )(*(pltpu.with_memory_space_constraint(a, pltpu.HBM) for a in (probes.reshape(flat), winds, diffusivity, mixing, prior_scale, obs_weight)))
    halo, first, second = call(
        merge_kernel, [(X_PARTS,) + tile, (Y_PARTS,) + tile, (Y_PARTS,) + tile]
    )(swap(edges, "gx", 0), swap(edges, "gx", 1), source, fields)
    second = swap(second, "gy", 1)
    first = swap(first, "gy", 0)
    field = (ROWS, LEVELS, 3) + tile
    derived = (2, DERIVED, ROWS, LANES)
    values = HALO * math.prod(field)
    inner, coefs = call(
        inner_kernel,
        [(HALO,) + field, derived],
        cost=pl.CostEstimate(flops=20 * values, bytes_accessed=8 * values, transcendentals=0),
    )(source, halo, fields)
    half = (HALO, LEVELS, 2) + tile
    width = PROBES * SLICES
    scratch = [
        pltpu.VMEM((HALO + 1, HALO, LEVELS, 3) + tile, F32),
        pltpu.VMEM((2, DERIVED, HALO, LANES), F32),
        pltpu.VMEM((HALO, width, LEVELS * LANES), jnp.bfloat16),
        pltpu.VMEM((2,) + tile, F32),
    ]
    near, high, low = call(
        near_kernel,
        [half, (width, width), (width, width)],
        scratch,
        cost=pl.CostEstimate(flops=20 * values, bytes_accessed=8 * values, transcendentals=0),
    )(inner, coefs, prior, first)
    far, message = call(far_kernel, [half, (size_y, 4, LANES)], scratch)(inner, coefs, prior, second, high, low)
    received = exchange(message, "gy")
    (message,) = call(sum_kernel, [(size_x, 4, LANES)])(received)
    received = exchange(message, "gx")
    basis, factor = call(
        lambda *refs: factor_kernel(count, *refs),
        [flat, (PROBES, PROBES)],
        [pltpu.VMEM(flat, F32), pltpu.SemaphoreType.DMA((LEVELS,))],
        spaces=[pltpu.HBM, pltpu.VMEM],
    )(received, near, far)
    return basis.reshape(probes.shape), factor


def solution(mesh):
    placed = (
        P(None, None, "gy", "gx"),
        P(None, None, "gy", "gx"),
        P(None, "gy", "gx"),
        P("gy", "gx"),
        P(None, "gy", "gx"),
        P(None, "gy", "gx"),
    )
    return jax.shard_map(
        body,
        mesh=mesh,
        in_specs=placed,
        out_specs=(P(None, None, "gy", "gx"), P()),
        check_vma=False,
    )
```

```python
import math
import jax
import jax.numpy as jnp
from jax import lax
from jax.experimental import pallas as pl
from jax.experimental.pallas import tpu as pltpu
from jax.sharding import PartitionSpec as P

STEPS = 4
LEVELS = 4
PROBES = 16
HALO = 2 * STEPS
LANES = 128
ROWS = 16
EXT = ROWS + 2 * HALO
F32 = jnp.float32

FIELDS = 17
GROUPS = 3
EAST, WEST, NORTH, SOUTH, CENTER, RATE, OBS, DERIVED = 0, 4, 8, 12, 16, 20, 21, 25
X_PARTS = ROWS + 2 * GROUPS
PAIRS = [(y, y + 8) for y in range(8)] + [(ROWS + 2 * group, ROWS + 2 * group + 1) for group in range(GROUPS)]
Y_SOURCE, Y_HALO, Y_COEF, Y_COEF_HALO, Y_PARTS = 0, 64, 72, 89, 92
SLICES = 4


def lane_ids():
    return lax.broadcasted_iota(jnp.int32, (8, LANES), 1)


def roll_lanes(value, shift):
    shift = shift % LANES
    return value if shift == 0 else pltpu.roll(value, shift, value.ndim - 1)


def pack_kernel(
    probes_in, winds_in, diffusivity_in, mixing_in, prior_in, obs_in,
    source, first, second, fields, prior, probes, edges, sems,
):
    coef_copies = [
        pltpu.make_async_copy(diffusivity_in, fields.at[pl.ds(0, 4)], sems.at[0]),
        pltpu.make_async_copy(winds_in.at[0], fields.at[pl.ds(4, 4)], sems.at[1]),
        pltpu.make_async_copy(winds_in.at[1], fields.at[pl.ds(8, 4)], sems.at[2]),
        pltpu.make_async_copy(obs_in, fields.at[pl.ds(12, 4)], sems.at[3]),
        pltpu.make_async_copy(mixing_in, fields.at[16], sems.at[4]),
    ]
    source_copies = [
        pltpu.make_async_copy(probes_in, probes, sems.at[5]),
        pltpu.make_async_copy(prior_in, prior, sems.at[6]),
    ]
    for copy in source_copies + coef_copies:
        copy.start()
    lanes = lane_ids()

    def put(held, value, slot):
        return jnp.where(lanes // 16 == slot, roll_lanes(value, 16 * slot + HALO), held)

    zero = jnp.zeros((8, LANES), F32)
    for copy in coef_copies:
        copy.wait()
    for group in range(GROUPS):
        for tile in range(2):
            held = zero
            for slot in range(8):
                field = 8 * group + slot
                if field < FIELDS:
                    held = put(held, fields[field, 8 * tile : 8 * tile + 8, :], slot)
            edges[ROWS + 2 * group + tile] = held
    for copy in source_copies:
        copy.wait()
    for y in range(ROWS):
        held = zero
        for level in range(LEVELS):
            scale = prior[level, y : y + 1, :]
            for part in range(2):
                value = probes[level, pl.ds(part * 8 * ROWS + y, 8, stride=ROWS), :] * scale
                source[y, level, part] = value
                held = put(held, value, 2 * level + part)
        edges[y] = held

    inner = lanes % 16 < 8
    odd_x = is_odd("gx")
    for index, (low, high) in enumerate(PAIRS):
        to_east = jnp.where(inner, edges[low], roll_lanes(edges[high], HALO))
        to_west = jnp.where(inner, roll_lanes(edges[high], -HALO), edges[low])
        first[index] = jnp.where(odd_x == 0, to_east, to_west)
        second[index] = jnp.where(odd_x == 0, to_west, to_east)


def is_odd(axis):
    return lax.axis_index(axis) % 2


def merge_kernel(first, second, source, fields, halo, first_out, second_out):
    inner = lane_ids() % 16 < 8
    odd_x, odd_y = is_odd("gx"), is_odd("gy")
    for index, (low, high) in enumerate(PAIRS):
        from_east = jnp.where(odd_x == 0, first[index], second[index])
        from_west = jnp.where(odd_x == 0, second[index], first[index])
        halo[low] = jnp.where(inner, roll_lanes(from_east, -HALO), roll_lanes(from_west, HALO))
        halo[high] = jnp.where(inner, from_east, from_west)
    for tile, out in ((1 - odd_y, first_out), (odd_y, second_out)):
        base = pl.multiple_of(8 * tile, 8)
        for y in range(8):
            for level in range(LEVELS):
                for part in range(2):
                    out[(y * LEVELS + level) * 2 + part] = source[base + y, level, part]
            out[Y_HALO + y] = halo[base + y]
        for field in range(FIELDS):
            out[Y_COEF + field] = fields[field, pl.ds(base, 8), :]
        for group in range(GROUPS):
            out[Y_COEF_HALO + group] = halo[ROWS + 2 * group + tile]


def strip_of(lanes, first, second, halo_first, halo_second, slot_first, slot_second):
    value = roll_lanes(first, 24)
    value = jnp.where(lanes >= 24, roll_lanes(halo_first, 24 - 16 * slot_first), value)
    value = jnp.where(lanes >= 40, roll_lanes(first, 40), value)
    value = jnp.where(lanes >= 64, roll_lanes(second, 88), value)
    value = jnp.where(lanes >= 88, roll_lanes(halo_second, 88 - 16 * slot_second), value)
    return jnp.where(lanes >= 104, roll_lanes(second, 104), value)


def two_sum(a, b):
    total = a + b
    other = total - a
    return total, (a - (total - other)) + (b - other)


def derive(coefs, rows, kind, values):
    rate = values[16]
    coefs[kind, RATE, rows, :] = rate
    for level in range(LEVELS):
        kappa, wind_x, wind_y = values[level], values[4 + level], values[8 + level]
        coefs[kind, EAST + level, rows, :] = kappa - wind_x
        coefs[kind, WEST + level, rows, :] = kappa + wind_x
        coefs[kind, NORTH + level, rows, :] = kappa - wind_y
        coefs[kind, SOUTH + level, rows, :] = kappa + wind_y
        sides = 1.0 if level in (0, LEVELS - 1) else 2.0
        coefs[kind, CENTER + level, rows, :] = 1.0 - 4.0 * kappa - sides * rate
        coefs[kind, OBS + level, rows, :] = values[12 + level]


def derive_both(coefs, tile, main, packed):
    lanes = lane_ids()
    strips = [
        strip_of(lanes, main[field], main[field], packed[field // 8], packed[field // 8], field % 8, field % 8)
        for field in range(FIELDS)
    ]
    for kind, values in ((0, main), (1, strips)):
        derive(coefs, slice(8 * tile, 8 * tile + 8), kind, values)


def vertical(values, level):
    if level == 0:
        return values[1]
    if level == LEVELS - 1:
        return values[LEVELS - 2]
    return values[level - 1] + values[level + 1]


def forward(get, coef_of, low, high, parts, emit):
    def load(y):
        return [[get(y, level, part) for level in range(LEVELS)] for part in parts]

    before, center = load(low - 1), load(low)
    for y in range(low, high):
        after = load(y + 1)
        coef = lambda index: coef_of(parts[0] // 2, index, y)
        rate = coef(RATE)
        results = [[None] * LEVELS for part in parts]
        for level in range(LEVELS):
            middle, east, west, north, south = [coef(base + level) for base in (CENTER, EAST, WEST, NORTH, SOUTH)]
            for index in range(len(parts)):
                value = center[index][level]
                results[index][level] = (
                    (middle * value + rate * vertical(center[index], level))
                    + (north * after[index][level] + south * before[index][level])
                    + (east * roll_lanes(value, -1) + west * roll_lanes(value, 1))
                )
        emit(y, parts, results)
        before, center = center, after


def adjoint(get, coef_of, low, high, parts, emit):
    def load(y):
        return [[get(y, level, part) for level in range(LEVELS)] for part in parts]

    def taken(base, y, values):
        own = [coef_of(parts[0] // 2, base + level, y) for level in range(LEVELS)]
        return [[own[level] * row[level] for level in range(LEVELS)] for row in values]

    pushed = taken(NORTH, low - 1, load(low - 1))
    partial = None
    for y in range(low, high + 1):
        center = load(y)
        if partial is not None:
            pulled = taken(SOUTH, y, center)
            emit(y - 1, parts, [
                [partial[index][level] + pulled[index][level] for level in range(LEVELS)] for index in range(len(parts))
            ])
        if y == high:
            break
        coef = lambda index: coef_of(parts[0] // 2, index, y)
        rate = coef(RATE)
        partial = [[None] * LEVELS for part in parts]
        for level in range(LEVELS):
            middle, east, west = [coef(base + level) for base in (CENTER, EAST, WEST)]
            for index in range(len(parts)):
                value = center[index][level]
                partial[index][level] = (
                    (middle * value + rate * vertical(center[index], level))
                    + (roll_lanes(west * value, -1) + roll_lanes(east * value, 1))
                    + pushed[index][level]
                )
        pushed = taken(NORTH, y, center)


GROUPED = ((2,), (0, 1))


def advance(step, low, high, get, put, coef_of):
    def emit(y, parts, results):
        for index, part in enumerate(parts):
            for level in range(LEVELS):
                value = results[index][level]
                if step < STEPS:
                    value = value + get(0, y, level, part)
                elif step == STEPS:
                    value = value * coef_of(part // 2, OBS + level, y)
                put(step, y, level, part, value)

    before = lambda y, level, part: get(step - 1, y, level, part)
    for parts in GROUPED:
        (forward if step <= STEPS else adjoint)(before, coef_of, low, high, parts, emit)


def inner_kernel(source, halo, fields, inner, coefs):
    lanes = lane_ids()
    for tile in range(2):
        main = [fields[field, 8 * tile : 8 * tile + 8, :] for field in range(FIELDS)]
        derive_both(coefs, tile, main, [halo[ROWS + 2 * group + tile] for group in range(GROUPS)])
    for y in range(ROWS):
        packed = halo[y]
        for level in range(LEVELS):
            low, high = source[y, level, 0], source[y, level, 1]
            inner[0, y, level, 0] = low
            inner[0, y, level, 1] = high
            inner[0, y, level, 2] = strip_of(lanes, low, high, packed, packed, 2 * level, 2 * level + 1)

    def get(step, y, level, part):
        return inner[step, y - HALO, level, part]

    def put(step, y, level, part, value):
        inner[step, y - HALO, level, part] = value

    def coef_of(kind, index, y):
        return coefs[kind, index, y - HALO : y - HALO + 1, :]

    for step in range(1, HALO):
        advance(step, HALO + step, HALO + ROWS - step, get, put, coef_of)


def side(tile, received, inner, coefs, prior, image, most_out, outer, outer_coefs):
    lanes = lane_ids()
    main = [received[Y_COEF + field] for field in range(FIELDS)]
    derive_both(outer_coefs, 0, main, [received[Y_COEF_HALO + group] for group in range(GROUPS)])
    for y in range(HALO):
        packed = received[Y_HALO + y]
        for level in range(LEVELS):
            low, high = received[(y * LEVELS + level) * 2], received[(y * LEVELS + level) * 2 + 1]
            outer[0, y, level, 0] = low
            outer[0, y, level, 1] = high
            outer[0, y, level, 2] = strip_of(lanes, low, high, packed, packed, 2 * level, 2 * level + 1)

    def first_row(step):
        return EXT - HALO - step if tile else step

    def place(step, y):
        base = first_row(step)
        return (outer, y - base) if base <= y < base + HALO else (inner, y - HALO)

    def get(step, y, level, part):
        ref, row = place(step, y)
        return ref[step, row, level, part]

    def put(step, y, level, part, value):
        ref, row = place(step, y)
        ref[step, row, level, part] = value

    def coef_of(kind, index, y):
        base = first_row(0)
        if base <= y < base + HALO:
            return outer_coefs[kind, index, y - base : y - base + 1, :]
        return coefs[kind, index, y - HALO : y - HALO + 1, :]

    for step in range(1, HALO):
        advance(step, first_row(step), first_row(step) + HALO, get, put, coef_of)

    most = [jnp.zeros((8, LANES), F32)] * 2
    last = first_row(HALO)

    def total_of(y, part, level, value):
        first, second, third = [get(step, y, level, part) for step in range(STEPS + 1, 2 * STEPS)]
        return (first + second) + (third + value)

    def emit_last(y, parts, results):
        for level in range(LEVELS):
            if parts == (2,):
                outer[HALO, y - last, level, 2] = total_of(y, 2, level, results[0][level])
                continue
            scale = prior[level, y - HALO : y - HALO + 1, :]
            strip = outer[HALO, y - last, level, 2]
            for part in parts:
                value = total_of(y, part, level, results[part][level])
                value = jnp.where(lanes < HALO, roll_lanes(strip, -40 - 64 * part), value)
                value = jnp.where(lanes >= LANES - HALO, roll_lanes(strip, 104 - 64 * part), value)
                value = value * scale
                image[y - last, level, part] = value
                most[part] = jnp.maximum(most[part], jnp.abs(value))

    for parts in GROUPED:
        adjoint(lambda y, level, part: get(HALO - 1, y, level, part), coef_of, last, last + HALO, parts, emit_last)
    for part in range(2):
        most_out[part] = most[part]


def both_sides(first, args):
    odd_y = is_odd("gy")
    for tile in range(2):
        @pl.when(odd_y == (1 - tile if first else tile))
        def _(tile=tile):
            side(tile, *args)


def gram_pieces(image, most, slices, high, low):
    magics = []
    for part in range(2):
        top = jnp.broadcast_to(jnp.max(most[part], axis=1, keepdims=True), (8, LANES))
        scaled = top * (2.0**23 + 1.0)
        power = jnp.abs(scaled - scaled * (1.0 - 2.0**-24))
        magics.append([power * (1.5 * 2.0 ** (23 - 6 - 8 * index)) for index in range(SLICES)])
    for y in range(HALO):
        for level in range(LEVELS):
            pieces = []
            for part in range(2):
                rest = image[y, level, part]
                own = []
                for index in range(SLICES):
                    magic = magics[part][index]
                    piece = (rest + magic) - magic
                    rest = rest - piece
                    own.append(piece)
                pieces.append(own)
            for index in range(SLICES):
                both = jnp.concatenate([pieces[0][index], pieces[1][index]], axis=0)
                slices[y, pl.ds(PROBES * index, PROBES), pl.ds(LANES * level, LANES)] = both.astype(jnp.bfloat16)
    for pair in range(HALO // 2):
        block = jnp.concatenate([slices[2 * pair], slices[2 * pair + 1]], axis=1)
        product = lax.dot_general(block, block, (((1,), (1,)), ((), ())), preferred_element_type=F32)
        high, error = two_sum(high, product)
        low = low + error
    return high, low


def near_kernel(inner, coefs, prior, received, image, high_out, low_out, outer, outer_coefs, slices, most):
    both_sides(True, (received, inner, coefs, prior, image, most, outer, outer_coefs))
    zero = jnp.zeros(high_out.shape, F32)
    high_out[...], low_out[...] = gram_pieces(image, most, slices, zero, zero)


def far_kernel(
    inner, coefs, prior, received, high_in, low_in, image, message, outer, outer_coefs, slices, most
):
    lanes = lane_ids()
    both_sides(False, (received, inner, coefs, prior, image, most, outer, outer_coefs))
    high, low = gram_pieces(image, most, slices, high_in[...], low_in[...])
    width = PROBES * SLICES

    def fold(high, low, blocks):
        total_high, total_low = None, None
        for block_high, block_low in blocks(high, low):
            if total_high is None:
                total_high, total_low = block_high, block_low
            else:
                total_high, error = two_sum(total_high, block_high)
                total_low = total_low + block_low + error
        return total_high, total_low

    def row_blocks(high, low):
        for index in range(SLICES):
            rows = slice(PROBES * index, PROBES * (index + 1))
            yield high[rows], low[rows]

    def lane_blocks(high, low):
        for index in range(SLICES):
            yield roll_lanes(high, -PROBES * index), roll_lanes(low, -PROBES * index)

    high, low = fold(high, low, row_blocks)
    rest = jnp.zeros((PROBES, LANES - width), F32)
    high, low = jnp.concatenate([high, rest], axis=1), jnp.concatenate([low, rest], axis=1)
    high, low = fold(high, low, lane_blocks)
    high, low = two_sum(high, low)

    wide = lax.broadcasted_iota(jnp.int32, (PROBES, LANES), 1)
    both = jnp.where(wide < PROBES, high, roll_lanes(low, PROBES))
    packed = both[0:8]
    for index in range(1, 4):
        value = both[8 * (index // 2) : 8 * (index // 2) + 8]
        if index % 2:
            value = pltpu.roll(value, 4, 0)
        packed = jnp.where(lanes // 32 == index, roll_lanes(value, 32 * index), packed)
    message[...] = jnp.broadcast_to(packed[None, 0:4], message.shape)


def split(a):
    scaled = a * 4097.0
    high = scaled - (scaled - a)
    return high, a - high


def product_error(a, b, product):
    a_high, a_low = a
    b_high, b_low = b
    return ((a_high * b_high - product) + a_high * b_low + a_low * b_high) + a_low * b_low


def summed(received):
    zero = jnp.zeros((8, LANES), F32)
    chains = 4
    sums, errors = [zero] * chains, [zero] * chains
    for index in range(received.shape[0]):
        chain = index % chains
        sums[chain], error = two_sum(sums[chain], received[index])
        errors[chain] = errors[chain] + error
    total, rest = sums[0], errors[0]
    for chain in range(1, chains):
        total, error = two_sum(total, sums[chain])
        rest = rest + errors[chain] + error
    total, error = two_sum(total, pltpu.roll(total, 4, 0))
    return total, rest + pltpu.roll(rest, 4, 0) + error


def sum_kernel(received, message):
    total, rest = summed(received)
    total = total + jnp.where(lane_ids() % 32 < PROBES, 0.0, roll_lanes(rest, PROBES))
    message[...] = jnp.broadcast_to(total[None, 0:4], message.shape)


def factor_kernel(count, received, near, far, basis, factor, held, sems):
    upper_half = lax.broadcasted_iota(jnp.int32, (8, LANES), 0) < 4
    total, rest = summed(received)
    rest = rest + roll_lanes(total, -PROBES)

    def unpack(value):
        low = jnp.where(upper_half, value, roll_lanes(value, -32))
        high = jnp.where(upper_half, roll_lanes(value, -64), roll_lanes(value, -96))
        return jnp.concatenate([low, high], axis=0)

    high, low = two_sum(unpack(total), unpack(rest))

    shape = (PROBES, LANES)
    wide = lax.broadcasted_iota(jnp.int32, shape, 1)
    rows = lax.broadcasted_iota(jnp.int32, shape, 0)
    high = jnp.where(wide < PROBES, high, jnp.where(wide == rows + PROBES, 1.0, 0.0))
    low = jnp.where(wide < PROBES, low, 0.0)

    def column(index):
        return [jnp.broadcast_to(value[:, index : index + 1], shape) for value in (high, low)]

    def row_of(value, index):
        return jnp.broadcast_to(value[index : index + 1], shape)

    own_high, own_low = column(0)
    for step in range(PROBES - 1):
        next_high, next_low = column(step + 1)
        pivot_high, pivot_low = row_of(own_high, step), row_of(own_low, step)
        inverse = 1.0 / pivot_high
        ratio = jnp.where(rows > step, own_high * inverse, 0.0)
        ratio_parts = split(ratio)
        taken = ratio * pivot_high
        remainder = ((own_high - taken) - product_error(ratio_parts, split(pivot_high), taken)) + (
            own_low - ratio * pivot_low
        )
        ratio_low = jnp.where(rows > step, remainder * inverse, 0.0)

        def reduce(high, low):
            row_high, row_low = row_of(high, step), row_of(low, step)
            taken = ratio * row_high
            error_taken = product_error(ratio_parts, split(row_high), taken)
            high, error = two_sum(high, -taken)
            low = low + error - error_taken - (ratio * row_low + ratio_low * row_high)
            return two_sum(high, low)

        own_high, own_low = reduce(next_high, next_low)
        high, low = reduce(high, low)

    diagonal = jnp.sum(jnp.where(wide == rows, high, 0.0), axis=1, keepdims=True)
    root = jnp.broadcast_to(jnp.sqrt(diagonal), shape)
    size = math.sqrt(count)
    upper = high / root
    factor[...] = jnp.where(wide >= rows, upper * (1.0 / size), 0.0)[:, :PROBES]
    inverse = upper * size
    columns = [
        jnp.broadcast_to(inverse[:, PROBES + index : PROBES + index + 1], shape) for index in range(PROBES)
    ]

    copies = []
    odd_y = is_odd("gy")
    for level in range(LEVELS):
        for image, base in ((near, 8 * (1 - odd_y)), (far, 8 * odd_y)):
            for y in range(HALO):
                outs = [None, None]
                for index in range(PROBES):
                    value = image[y, level, index // 8, index % 8 : index % 8 + 1, :]
                    for part in range(index // 8, 2):
                        term = columns[index][8 * part : 8 * part + 8] * value
                        outs[part] = term if outs[part] is None else outs[part] + term
                for part in range(2):
                    held[level, pl.ds(base + (part * 8 * ROWS + y), 8, stride=ROWS), :] = outs[part]
        copies.append(pltpu.make_async_copy(held.at[level], basis.at[level], sems.at[level]))
        copies[-1].start()
    for copy in copies:
        copy.wait()


def call(kernel, outs, scratch=(), inputs=pltpu.VMEM, spaces=None, cost=None):
    def run(*operands):
        return pl.pallas_call(
            kernel,
            out_shape=[jax.ShapeDtypeStruct(shape, F32) for shape in outs],
            in_specs=[pl.BlockSpec(memory_space=inputs)] * len(operands),
            out_specs=[pl.BlockSpec(memory_space=space) for space in spaces or [pltpu.VMEM] * len(outs)],
            scratch_shapes=list(scratch),
            cost_estimate=cost,
            compiler_params=pltpu.CompilerParams(vmem_limit_bytes=40 << 20),
        )(*operands)

    return run


def body(probes, winds, diffusivity, mixing, prior_scale, obs_weight):
    tile = (8, LANES)
    size_x, size_y = lax.axis_size("gx"), lax.axis_size("gy")
    count = LEVELS * ROWS * LANES * size_x * size_y

    def swap(value, axis, start):
        pairs = [(i, i + 1) for i in range(start, lax.axis_size(axis) - 1, 2)]
        return lax.ppermute(value, axis, pairs + [(j, i) for i, j in pairs])

    def exchange(message, axis):
        received = lax.all_to_all(message, axis, 0, 0)
        return received.reshape((message.shape[0] // 2,) + tile)

    flat = (LEVELS, PROBES * ROWS, LANES)
    source, first, second, fields, prior = call(
        pack_kernel,
        [(ROWS, LEVELS, 2) + tile, (len(PAIRS),) + tile, (len(PAIRS),) + tile, (FIELDS, ROWS, LANES), (LEVELS, ROWS, LANES)],
        [pltpu.VMEM(flat, F32), pltpu.VMEM((X_PARTS,) + tile, F32), pltpu.SemaphoreType.DMA((7,))],
        pltpu.HBM,
    )(*(pltpu.with_memory_space_constraint(a, pltpu.HBM) for a in (probes.reshape(flat), winds, diffusivity, mixing, prior_scale, obs_weight)))
    halo, first, second = call(
        merge_kernel, [(X_PARTS,) + tile, (Y_PARTS,) + tile, (Y_PARTS,) + tile]
    )(swap(first, "gx", 0), swap(second, "gx", 1), source, fields)
    second = swap(second, "gy", 1)
    first = swap(first, "gy", 0)
    field = (ROWS, LEVELS, 3) + tile
    derived = (2, DERIVED, ROWS, LANES)
    values = HALO * math.prod(field)
    inner, coefs = call(
        inner_kernel,
        [(HALO,) + field, derived],
        cost=pl.CostEstimate(flops=20 * values, bytes_accessed=8 * values, transcendentals=0),
    )(source, halo, fields)
    half = (HALO, LEVELS, 2) + tile
    width = PROBES * SLICES
    scratch = [
        pltpu.VMEM((HALO + 1, HALO, LEVELS, 3) + tile, F32),
        pltpu.VMEM((2, DERIVED, HALO, LANES), F32),
        pltpu.VMEM((HALO, width, LEVELS * LANES), jnp.bfloat16),
        pltpu.VMEM((2,) + tile, F32),
    ]
    near, high, low = call(
        near_kernel,
        [half, (width, width), (width, width)],
        scratch,
        cost=pl.CostEstimate(flops=20 * values, bytes_accessed=8 * values, transcendentals=0),
    )(inner, coefs, prior, first)
    far, message = call(far_kernel, [half, (size_y, 4, LANES)], scratch)(inner, coefs, prior, second, high, low)
    received = exchange(message, "gy")
    (message,) = call(sum_kernel, [(size_x, 4, LANES)])(received)
    received = exchange(message, "gx")
    basis, factor = call(
        lambda *refs: factor_kernel(count, *refs),
        [flat, (PROBES, PROBES)],
        [pltpu.VMEM(flat, F32), pltpu.SemaphoreType.DMA((LEVELS,))],
        spaces=[pltpu.HBM, pltpu.VMEM],
    )(received, near, far)
    return basis.reshape(probes.shape), factor


def solution(mesh):
    placed = (
        P(None, None, "gy", "gx"),
        P(None, None, "gy", "gx"),
        P(None, "gy", "gx"),
        P("gy", "gx"),
        P(None, "gy", "gx"),
        P(None, "gy", "gx"),
    )
    return jax.shard_map(
        body,
        mesh=mesh,
        in_specs=placed,
        out_specs=(P(None, None, "gy", "gx"), P()),
        check_vma=False,
    )
```

```python
import math
import jax
import jax.numpy as jnp
from jax import lax
from jax.experimental import pallas as pl
from jax.experimental.pallas import tpu as pltpu
from jax.sharding import PartitionSpec as P

STEPS = 4
LEVELS = 4
PROBES = 16
HALO = 2 * STEPS
LANES = 128
ROWS = 16
EXT = ROWS + 2 * HALO
F32 = jnp.float32

FIELDS = 17
GROUPS = 3
EAST, WEST, NORTH, SOUTH, CENTER, RATE, OBS, DERIVED = 0, 4, 8, 12, 16, 20, 21, 25
X_PARTS = ROWS + 2 * GROUPS
PAIRS = [(y, y + 8) for y in range(8)] + [(ROWS + 2 * group, ROWS + 2 * group + 1) for group in range(GROUPS)]
Y_SOURCE, Y_HALO, Y_COEF, Y_COEF_HALO, Y_PARTS = 0, 64, 72, 89, 92
SLICES = 4


def lane_ids():
    return lax.broadcasted_iota(jnp.int32, (8, LANES), 1)


def roll_lanes(value, shift):
    shift = shift % LANES
    return value if shift == 0 else pltpu.roll(value, shift, value.ndim - 1)


def pack_kernel(
    probes_in, winds_in, diffusivity_in, mixing_in, prior_in, obs_in,
    source, second, first, fields, prior, probes, edges, sems,
):
    coef_copies = [
        pltpu.make_async_copy(diffusivity_in, fields.at[pl.ds(0, 4)], sems.at[0]),
        pltpu.make_async_copy(winds_in.at[0], fields.at[pl.ds(4, 4)], sems.at[1]),
        pltpu.make_async_copy(winds_in.at[1], fields.at[pl.ds(8, 4)], sems.at[2]),
        pltpu.make_async_copy(obs_in, fields.at[pl.ds(12, 4)], sems.at[3]),
        pltpu.make_async_copy(mixing_in, fields.at[16], sems.at[4]),
    ]
    source_copies = [
        pltpu.make_async_copy(probes_in, probes, sems.at[5]),
        pltpu.make_async_copy(prior_in, prior, sems.at[6]),
    ]
    for copy in source_copies + coef_copies:
        copy.start()
    lanes = lane_ids()

    def put(held, value, slot):
        return jnp.where(lanes // 16 == slot, roll_lanes(value, 16 * slot + HALO), held)

    zero = jnp.zeros((8, LANES), F32)
    for copy in coef_copies:
        copy.wait()
    for group in range(GROUPS):
        for tile in range(2):
            held = zero
            for slot in range(8):
                field = 8 * group + slot
                if field < FIELDS:
                    held = put(held, fields[field, 8 * tile : 8 * tile + 8, :], slot)
            edges[ROWS + 2 * group + tile] = held
    for copy in source_copies:
        copy.wait()
    for y in range(ROWS):
        held = zero
        for level in range(LEVELS):
            scale = prior[level, y : y + 1, :]
            for part in range(2):
                value = probes[level, pl.ds(part * 8 * ROWS + y, 8, stride=ROWS), :] * scale
                source[y, level, part] = value
                held = put(held, value, 2 * level + part)
        edges[y] = held

    inner = lanes % 16 < 8
    odd_x = is_odd("gx")
    for index, (low, high) in enumerate(PAIRS):
        to_east = jnp.where(inner, edges[low], roll_lanes(edges[high], HALO))
        to_west = jnp.where(inner, roll_lanes(edges[high], -HALO), edges[low])
        first[index] = jnp.where(odd_x == 0, to_east, to_west)
        second[index] = jnp.where(odd_x == 0, to_west, to_east)


def is_odd(axis):
    return lax.axis_index(axis) % 2


def merge_kernel(second, first, source, fields, halo, first_out, second_out):
    inner = lane_ids() % 16 < 8
    odd_x, odd_y = is_odd("gx"), is_odd("gy")
    for index, (low, high) in enumerate(PAIRS):
        from_east = jnp.where(odd_x == 0, first[index], second[index])
        from_west = jnp.where(odd_x == 0, second[index], first[index])
        halo[low] = jnp.where(inner, roll_lanes(from_east, -HALO), roll_lanes(from_west, HALO))
        halo[high] = jnp.where(inner, from_east, from_west)
    for tile, out in ((1 - odd_y, first_out), (odd_y, second_out)):
        base = pl.multiple_of(8 * tile, 8)
        for y in range(8):
            for level in range(LEVELS):
                for part in range(2):
                    out[(y * LEVELS + level) * 2 + part] = source[base + y, level, part]
            out[Y_HALO + y] = halo[base + y]
        for field in range(FIELDS):
            out[Y_COEF + field] = fields[field, pl.ds(base, 8), :]
        for group in range(GROUPS):
            out[Y_COEF_HALO + group] = halo[ROWS + 2 * group + tile]


def strip_of(lanes, first, second, halo_first, halo_second, slot_first, slot_second):
    value = roll_lanes(first, 24)
    value = jnp.where(lanes >= 24, roll_lanes(halo_first, 24 - 16 * slot_first), value)
    value = jnp.where(lanes >= 40, roll_lanes(first, 40), value)
    value = jnp.where(lanes >= 64, roll_lanes(second, 88), value)
    value = jnp.where(lanes >= 88, roll_lanes(halo_second, 88 - 16 * slot_second), value)
    return jnp.where(lanes >= 104, roll_lanes(second, 104), value)


def two_sum(a, b):
    total = a + b
    other = total - a
    return total, (a - (total - other)) + (b - other)


def derive(coefs, rows, kind, values):
    rate = values[16]
    coefs[kind, RATE, rows, :] = rate
    for level in range(LEVELS):
        kappa, wind_x, wind_y = values[level], values[4 + level], values[8 + level]
        coefs[kind, EAST + level, rows, :] = kappa - wind_x
        coefs[kind, WEST + level, rows, :] = kappa + wind_x
        coefs[kind, NORTH + level, rows, :] = kappa - wind_y
        coefs[kind, SOUTH + level, rows, :] = kappa + wind_y
        sides = 1.0 if level in (0, LEVELS - 1) else 2.0
        coefs[kind, CENTER + level, rows, :] = 1.0 - 4.0 * kappa - sides * rate
        coefs[kind, OBS + level, rows, :] = values[12 + level]


def derive_both(coefs, tile, main, packed):
    lanes = lane_ids()
    strips = [
        strip_of(lanes, main[field], main[field], packed[field // 8], packed[field // 8], field % 8, field % 8)
        for field in range(FIELDS)
    ]
    for kind, values in ((0, main), (1, strips)):
        derive(coefs, slice(8 * tile, 8 * tile + 8), kind, values)


def vertical(values, level):
    if level == 0:
        return values[1]
    if level == LEVELS - 1:
        return values[LEVELS - 2]
    return values[level - 1] + values[level + 1]


def forward(get, coef_of, low, high, parts, emit):
    def load(y):
        return [[get(y, level, part) for level in range(LEVELS)] for part in parts]

    before, center = load(low - 1), load(low)
    for y in range(low, high):
        after = load(y + 1)
        coef = lambda index: coef_of(parts[0] // 2, index, y)
        rate = coef(RATE)
        results = [[None] * LEVELS for part in parts]
        for level in range(LEVELS):
            middle, east, west, north, south = [coef(base + level) for base in (CENTER, EAST, WEST, NORTH, SOUTH)]
            for index in range(len(parts)):
                value = center[index][level]
                results[index][level] = (
                    (middle * value + rate * vertical(center[index], level))
                    + (north * after[index][level] + south * before[index][level])
                    + (east * roll_lanes(value, -1) + west * roll_lanes(value, 1))
                )
        emit(y, parts, results)
        before, center = center, after


def adjoint(get, coef_of, low, high, parts, emit):
    def load(y):
        return [[get(y, level, part) for level in range(LEVELS)] for part in parts]

    def taken(base, y, values):
        own = [coef_of(parts[0] // 2, base + level, y) for level in range(LEVELS)]
        return [[own[level] * row[level] for level in range(LEVELS)] for row in values]

    pushed = taken(NORTH, low - 1, load(low - 1))
    partial = None
    for y in range(low, high + 1):
        center = load(y)
        if partial is not None:
            pulled = taken(SOUTH, y, center)
            emit(y - 1, parts, [
                [partial[index][level] + pulled[index][level] for level in range(LEVELS)] for index in range(len(parts))
            ])
        if y == high:
            break
        coef = lambda index: coef_of(parts[0] // 2, index, y)
        rate = coef(RATE)
        partial = [[None] * LEVELS for part in parts]
        for level in range(LEVELS):
            middle, east, west = [coef(base + level) for base in (CENTER, EAST, WEST)]
            for index in range(len(parts)):
                value = center[index][level]
                partial[index][level] = (
                    (middle * value + rate * vertical(center[index], level))
                    + (roll_lanes(west * value, -1) + roll_lanes(east * value, 1))
                    + pushed[index][level]
                )
        pushed = taken(NORTH, y, center)


GROUPED = ((2,), (0, 1))


def advance(step, low, high, get, put, coef_of):
    def emit(y, parts, results):
        for index, part in enumerate(parts):
            for level in range(LEVELS):
                value = results[index][level]
                if step < STEPS:
                    value = value + get(0, y, level, part)
                elif step == STEPS:
                    value = value * coef_of(part // 2, OBS + level, y)
                put(step, y, level, part, value)

    before = lambda y, level, part: get(step - 1, y, level, part)
    for parts in GROUPED:
        (forward if step <= STEPS else adjoint)(before, coef_of, low, high, parts, emit)


def inner_kernel(source, halo, fields, inner, coefs):
    lanes = lane_ids()
    for tile in range(2):
        main = [fields[field, 8 * tile : 8 * tile + 8, :] for field in range(FIELDS)]
        derive_both(coefs, tile, main, [halo[ROWS + 2 * group + tile] for group in range(GROUPS)])
    for y in range(ROWS):
        packed = halo[y]
        for level in range(LEVELS):
            low, high = source[y, level, 0], source[y, level, 1]
            inner[0, y, level, 0] = low
            inner[0, y, level, 1] = high
            inner[0, y, level, 2] = strip_of(lanes, low, high, packed, packed, 2 * level, 2 * level + 1)

    def get(step, y, level, part):
        return inner[step, y - HALO, level, part]

    def put(step, y, level, part, value):
        inner[step, y - HALO, level, part] = value

    def coef_of(kind, index, y):
        return coefs[kind, index, y - HALO : y - HALO + 1, :]

    for step in range(1, HALO):
        advance(step, HALO + step, HALO + ROWS - step, get, put, coef_of)


def side(tile, received, inner, coefs, prior, image, most_out, outer, outer_coefs):
    lanes = lane_ids()
    main = [received[Y_COEF + field] for field in range(FIELDS)]
    derive_both(outer_coefs, 0, main, [received[Y_COEF_HALO + group] for group in range(GROUPS)])
    for y in range(HALO):
        packed = received[Y_HALO + y]
        for level in range(LEVELS):
            low, high = received[(y * LEVELS + level) * 2], received[(y * LEVELS + level) * 2 + 1]
            outer[0, y, level, 0] = low
            outer[0, y, level, 1] = high
            outer[0, y, level, 2] = strip_of(lanes, low, high, packed, packed, 2 * level, 2 * level + 1)

    def first_row(step):
        return EXT - HALO - step if tile else step

    def place(step, y):
        base = first_row(step)
        return (outer, y - base) if base <= y < base + HALO else (inner, y - HALO)

    def get(step, y, level, part):
        ref, row = place(step, y)
        return ref[step, row, level, part]

    def put(step, y, level, part, value):
        ref, row = place(step, y)
        ref[step, row, level, part] = value

    def coef_of(kind, index, y):
        base = first_row(0)
        if base <= y < base + HALO:
            return outer_coefs[kind, index, y - base : y - base + 1, :]
        return coefs[kind, index, y - HALO : y - HALO + 1, :]

    for step in range(1, HALO):
        advance(step, first_row(step), first_row(step) + HALO, get, put, coef_of)

    most = [jnp.zeros((8, LANES), F32)] * 2
    last = first_row(HALO)

    def total_of(y, part, level, value):
        first, second, third = [get(step, y, level, part) for step in range(STEPS + 1, 2 * STEPS)]
        return (first + second) + (third + value)

    def emit_last(y, parts, results):
        for level in range(LEVELS):
            if parts == (2,):
                outer[HALO, y - last, level, 2] = total_of(y, 2, level, results[0][level])
                continue
            scale = prior[level, y - HALO : y - HALO + 1, :]
            strip = outer[HALO, y - last, level, 2]
            for part in parts:
                value = total_of(y, part, level, results[part][level])
                value = jnp.where(lanes < HALO, roll_lanes(strip, -40 - 64 * part), value)
                value = jnp.where(lanes >= LANES - HALO, roll_lanes(strip, 104 - 64 * part), value)
                value = value * scale
                image[y - last, level, part] = value
                most[part] = jnp.maximum(most[part], jnp.abs(value))

    for parts in GROUPED:
        adjoint(lambda y, level, part: get(HALO - 1, y, level, part), coef_of, last, last + HALO, parts, emit_last)
    for part in range(2):
        most_out[part] = most[part]


def both_sides(first, args):
    odd_y = is_odd("gy")
    for tile in range(2):
        @pl.when(odd_y == (1 - tile if first else tile))
        def _(tile=tile):
            side(tile, *args)


def gram_pieces(image, most, slices, high, low):
    magics = []
    for part in range(2):
        top = jnp.broadcast_to(jnp.max(most[part], axis=1, keepdims=True), (8, LANES))
        scaled = top * (2.0**23 + 1.0)
        power = jnp.abs(scaled - scaled * (1.0 - 2.0**-24))
        magics.append([power * (1.5 * 2.0 ** (23 - 6 - 8 * index)) for index in range(SLICES)])
    for y in range(HALO):
        for level in range(LEVELS):
            pieces = []
            for part in range(2):
                rest = image[y, level, part]
                own = []
                for index in range(SLICES):
                    magic = magics[part][index]
                    piece = (rest + magic) - magic
                    rest = rest - piece
                    own.append(piece)
                pieces.append(own)
            for index in range(SLICES):
                both = jnp.concatenate([pieces[0][index], pieces[1][index]], axis=0)
                slices[y, pl.ds(PROBES * index, PROBES), pl.ds(LANES * level, LANES)] = both.astype(jnp.bfloat16)
    for pair in range(HALO // 2):
        block = jnp.concatenate([slices[2 * pair], slices[2 * pair + 1]], axis=1)
        product = lax.dot_general(block, block, (((1,), (1,)), ((), ())), preferred_element_type=F32)
        high, error = two_sum(high, product)
        low = low + error
    return high, low


def near_kernel(inner, coefs, prior, received, image, high_out, low_out, outer, outer_coefs, slices, most):
    both_sides(True, (received, inner, coefs, prior, image, most, outer, outer_coefs))
    zero = jnp.zeros(high_out.shape, F32)
    high_out[...], low_out[...] = gram_pieces(image, most, slices, zero, zero)


def far_kernel(
    inner, coefs, prior, received, high_in, low_in, image, message, outer, outer_coefs, slices, most
):
    lanes = lane_ids()
    both_sides(False, (received, inner, coefs, prior, image, most, outer, outer_coefs))
    high, low = gram_pieces(image, most, slices, high_in[...], low_in[...])
    width = PROBES * SLICES

    def fold(high, low, blocks):
        total_high, total_low = None, None
        for block_high, block_low in blocks(high, low):
            if total_high is None:
                total_high, total_low = block_high, block_low
            else:
                total_high, error = two_sum(total_high, block_high)
                total_low = total_low + block_low + error
        return total_high, total_low

    def row_blocks(high, low):
        for index in range(SLICES):
            rows = slice(PROBES * index, PROBES * (index + 1))
            yield high[rows], low[rows]

    def lane_blocks(high, low):
        for index in range(SLICES):
            yield roll_lanes(high, -PROBES * index), roll_lanes(low, -PROBES * index)

    high, low = fold(high, low, row_blocks)
    rest = jnp.zeros((PROBES, LANES - width), F32)
    high, low = jnp.concatenate([high, rest], axis=1), jnp.concatenate([low, rest], axis=1)
    high, low = fold(high, low, lane_blocks)
    high, low = two_sum(high, low)

    wide = lax.broadcasted_iota(jnp.int32, (PROBES, LANES), 1)
    both = jnp.where(wide < PROBES, high, roll_lanes(low, PROBES))
    packed = both[0:8]
    for index in range(1, 4):
        value = both[8 * (index // 2) : 8 * (index // 2) + 8]
        if index % 2:
            value = pltpu.roll(value, 4, 0)
        packed = jnp.where(lanes // 32 == index, roll_lanes(value, 32 * index), packed)
    message[...] = jnp.broadcast_to(packed[None, 0:4], message.shape)


def split(a):
    scaled = a * 4097.0
    high = scaled - (scaled - a)
    return high, a - high


def product_error(a, b, product):
    a_high, a_low = a
    b_high, b_low = b
    return ((a_high * b_high - product) + a_high * b_low + a_low * b_high) + a_low * b_low


def summed(received):
    zero = jnp.zeros((8, LANES), F32)
    chains = 4
    sums, errors = [zero] * chains, [zero] * chains
    for index in range(received.shape[0]):
        chain = index % chains
        sums[chain], error = two_sum(sums[chain], received[index])
        errors[chain] = errors[chain] + error
    total, rest = sums[0], errors[0]
    for chain in range(1, chains):
        total, error = two_sum(total, sums[chain])
        rest = rest + errors[chain] + error
    total, error = two_sum(total, pltpu.roll(total, 4, 0))
    return total, rest + pltpu.roll(rest, 4, 0) + error


def sum_kernel(received, message):
    total, rest = summed(received)
    total = total + jnp.where(lane_ids() % 32 < PROBES, 0.0, roll_lanes(rest, PROBES))
    message[...] = jnp.broadcast_to(total[None, 0:4], message.shape)


def factor_kernel(count, received, near, far, basis, factor, held, sems):
    upper_half = lax.broadcasted_iota(jnp.int32, (8, LANES), 0) < 4
    total, rest = summed(received)
    rest = rest + roll_lanes(total, -PROBES)

    def unpack(value):
        low = jnp.where(upper_half, value, roll_lanes(value, -32))
        high = jnp.where(upper_half, roll_lanes(value, -64), roll_lanes(value, -96))
        return jnp.concatenate([low, high], axis=0)

    high, low = two_sum(unpack(total), unpack(rest))

    shape = (PROBES, LANES)
    wide = lax.broadcasted_iota(jnp.int32, shape, 1)
    rows = lax.broadcasted_iota(jnp.int32, shape, 0)
    high = jnp.where(wide < PROBES, high, jnp.where(wide == rows + PROBES, 1.0, 0.0))
    low = jnp.where(wide < PROBES, low, 0.0)

    def column(index):
        return [jnp.broadcast_to(value[:, index : index + 1], shape) for value in (high, low)]

    def row_of(value, index):
        return jnp.broadcast_to(value[index : index + 1], shape)

    own_high, own_low = column(0)
    for step in range(PROBES - 1):
        next_high, next_low = column(step + 1)
        pivot_high, pivot_low = row_of(own_high, step), row_of(own_low, step)
        inverse = 1.0 / pivot_high
        ratio = jnp.where(rows > step, own_high * inverse, 0.0)
        ratio_parts = split(ratio)
        taken = ratio * pivot_high
        remainder = ((own_high - taken) - product_error(ratio_parts, split(pivot_high), taken)) + (
            own_low - ratio * pivot_low
        )
        ratio_low = jnp.where(rows > step, remainder * inverse, 0.0)

        def reduce(high, low):
            row_high, row_low = row_of(high, step), row_of(low, step)
            taken = ratio * row_high
            error_taken = product_error(ratio_parts, split(row_high), taken)
            high, error = two_sum(high, -taken)
            low = low + error - error_taken - (ratio * row_low + ratio_low * row_high)
            return two_sum(high, low)

        own_high, own_low = reduce(next_high, next_low)
        high, low = reduce(high, low)

    diagonal = jnp.sum(jnp.where(wide == rows, high, 0.0), axis=1, keepdims=True)
    root = jnp.broadcast_to(jnp.sqrt(diagonal), shape)
    size = math.sqrt(count)
    upper = high / root
    factor[...] = jnp.where(wide >= rows, upper * (1.0 / size), 0.0)[:, :PROBES]
    inverse = upper * size
    columns = [
        jnp.broadcast_to(inverse[:, PROBES + index : PROBES + index + 1], shape) for index in range(PROBES)
    ]

    copies = []
    odd_y = is_odd("gy")
    for level in range(LEVELS):
        for image, base in ((near, 8 * (1 - odd_y)), (far, 8 * odd_y)):
            for y in range(HALO):
                outs = [None, None]
                for index in range(PROBES):
                    value = image[y, level, index // 8, index % 8 : index % 8 + 1, :]
                    for part in range(index // 8, 2):
                        term = columns[index][8 * part : 8 * part + 8] * value
                        outs[part] = term if outs[part] is None else outs[part] + term
                for part in range(2):
                    held[level, pl.ds(base + (part * 8 * ROWS + y), 8, stride=ROWS), :] = outs[part]
        copies.append(pltpu.make_async_copy(held.at[level], basis.at[level], sems.at[level]))
        copies[-1].start()
    for copy in copies:
        copy.wait()


def call(kernel, outs, scratch=(), inputs=pltpu.VMEM, spaces=None, cost=None):
    def run(*operands):
        return pl.pallas_call(
            kernel,
            out_shape=[jax.ShapeDtypeStruct(shape, F32) for shape in outs],
            in_specs=[pl.BlockSpec(memory_space=inputs)] * len(operands),
            out_specs=[pl.BlockSpec(memory_space=space) for space in spaces or [pltpu.VMEM] * len(outs)],
            scratch_shapes=list(scratch),
            cost_estimate=cost,
            compiler_params=pltpu.CompilerParams(vmem_limit_bytes=40 << 20),
        )(*operands)

    return run


def body(probes, winds, diffusivity, mixing, prior_scale, obs_weight):
    tile = (8, LANES)
    size_x, size_y = lax.axis_size("gx"), lax.axis_size("gy")
    count = LEVELS * ROWS * LANES * size_x * size_y

    def swap(value, axis, start):
        pairs = [(i, i + 1) for i in range(start, lax.axis_size(axis) - 1, 2)]
        return lax.ppermute(value, axis, pairs + [(j, i) for i, j in pairs])

    def exchange(message, axis):
        received = lax.all_to_all(message, axis, 0, 0)
        return received.reshape((message.shape[0] // 2,) + tile)

    flat = (LEVELS, PROBES * ROWS, LANES)
    source, second, first, fields, prior = call(
        pack_kernel,
        [(ROWS, LEVELS, 2) + tile, (len(PAIRS),) + tile, (len(PAIRS),) + tile, (FIELDS, ROWS, LANES), (LEVELS, ROWS, LANES)],
        [pltpu.VMEM(flat, F32), pltpu.VMEM((X_PARTS,) + tile, F32), pltpu.SemaphoreType.DMA((7,))],
        pltpu.HBM,
    )(*(pltpu.with_memory_space_constraint(a, pltpu.HBM) for a in (probes.reshape(flat), winds, diffusivity, mixing, prior_scale, obs_weight)))
    halo, first, second = call(
        merge_kernel, [(X_PARTS,) + tile, (Y_PARTS,) + tile, (Y_PARTS,) + tile]
    )(swap(second, "gx", 1), swap(first, "gx", 0), source, fields)
    second = swap(second, "gy", 1)
    first = swap(first, "gy", 0)
    field = (ROWS, LEVELS, 3) + tile
    derived = (2, DERIVED, ROWS, LANES)
    values = HALO * math.prod(field)
    inner, coefs = call(
        inner_kernel,
        [(HALO,) + field, derived],
        cost=pl.CostEstimate(flops=20 * values, bytes_accessed=8 * values, transcendentals=0),
    )(source, halo, fields)
    half = (HALO, LEVELS, 2) + tile
    width = PROBES * SLICES
    scratch = [
        pltpu.VMEM((HALO + 1, HALO, LEVELS, 3) + tile, F32),
        pltpu.VMEM((2, DERIVED, HALO, LANES), F32),
        pltpu.VMEM((HALO, width, LEVELS * LANES), jnp.bfloat16),
        pltpu.VMEM((2,) + tile, F32),
    ]
    near, high, low = call(
        near_kernel,
        [half, (width, width), (width, width)],
        scratch,
        cost=pl.CostEstimate(flops=20 * values, bytes_accessed=8 * values, transcendentals=0),
    )(inner, coefs, prior, first)
    far, message = call(far_kernel, [half, (size_y, 4, LANES)], scratch)(inner, coefs, prior, second, high, low)
    received = exchange(message, "gy")
    (message,) = call(sum_kernel, [(size_x, 4, LANES)])(received)
    received = exchange(message, "gx")
    basis, factor = call(
        lambda *refs: factor_kernel(count, *refs),
        [flat, (PROBES, PROBES)],
        [pltpu.VMEM(flat, F32), pltpu.SemaphoreType.DMA((LEVELS,))],
        spaces=[pltpu.HBM, pltpu.VMEM],
    )(received, near, far)
    return basis.reshape(probes.shape), factor


def solution(mesh):
    placed = (
        P(None, None, "gy", "gx"),
        P(None, None, "gy", "gx"),
        P(None, "gy", "gx"),
        P("gy", "gx"),
        P(None, "gy", "gx"),
        P(None, "gy", "gx"),
    )
    return jax.shard_map(
        body,
        mesh=mesh,
        in_specs=placed,
        out_specs=(P(None, None, "gy", "gx"), P()),
        check_vma=False,
    )
```
